128 devices in a mesh: fsdp: 16 (over x, z_lo, core), tp: 8 (over y, z_hi).
Axes of the slice: x: 4, y: 4, z: 4 (z_hi: 2, z_lo: 2; z = z_hi * 2 + z_lo), core: 2. Of those that a mesh axis runs over, the one named last changes fastest.
Arguments:
- tokens: bfloat16 [20480, 1024], P(('fsdp', 'tp')), may hold values from -6 to 6
- gain_attn: float32 [1024], replicated, may hold values from 0.25 to 1.75
- w_qkv: bfloat16 [1024, 3, 1024], P('fsdp', None, 'tp'), may hold values from -0.1875 to 0.1875
- w_out: bfloat16 [1024, 1024], P('fsdp', 'tp'), may hold values from -6 to 6
- gain_mlp: float32 [1024], replicated, may hold values from 0.25 to 1.75
- w_in: bfloat16 [1024, 2, 2624], P('fsdp', None, 'tp'), may hold values from -0.1875 to 0.1875
- w_down: bfloat16 [1024, 2624], P('fsdp', 'tp'), may hold values from -0.125 to 0.125
- cotangent: bfloat16 [20480, 1024], P(('fsdp', 'tp')), may hold values from -6 to 6
Outputs:
- layer_out: bfloat16 [20480, 1024], P(('fsdp', 'tp'))
- grad_tokens: bfloat16 [20480, 1024], P(('fsdp', 'tp'))
- grad_gain_attn: float32 [1024], replicated
- grad_w_qkv: float32 [1024, 3, 1024], P('fsdp', None, 'tp')
- grad_w_out: float32 [1024, 1024], P('fsdp', 'tp')
- grad_gain_mlp: float32 [1024], replicated
- grad_w_in: float32 [1024, 2, 2624], P('fsdp', None, 'tp')
- grad_w_down: float32 [1024, 2624], P('fsdp', 'tp')
The draws below stay inside these ranges and needn't reach their ends.
All inputs are finite; a program needn't handle non-finite values.
Results may differ from the reference program's by a relative error of at most 0.029.
Values may be sent and summed in bfloat16 or wider, within the bound.
No kernel may reach another device: no remote copies, remote signals or barrier semaphores. Data moves between devices by JAX's collectives and lax.ppermute only.
A program may use at most 128 MiB of HBM per device.

```python
import jax
import jax.numpy as jnp
from jax import lax

D = 1024
H = 16
HD = 64
FF = 2624
LEN = 1280
TOKENS = 20480


def levels(own_key, extent, cuts, smallest, largest):
    level = 1.0
    for axis_at, blocks in cuts:
        steps = jax.random.uniform(jax.random.fold_in(jax.random.fold_in(own_key, 6), axis_at), (blocks,), jnp.float32, smallest / len(cuts), largest / len(cuts))
        level = level * jnp.repeat(jnp.exp(steps), extent[axis_at] // blocks).reshape((-1,) + (1,) * (len(extent) - 1 - axis_at))
    return level


def scatter_about(rng, dims, deviation, reach, split=(), kind=jnp.bfloat16):
    array = jax.random.normal(rng, dims, jnp.float32) * deviation
    if len(split) > 0:
        array = levels(rng, dims, split, -0.22, 0.18) * array
    return jnp.clip(array, min=-reach, max=reach).astype(kind)


def setup_inputs(seed: int = 0) -> dict:
    seeds = jax.random.split(jax.random.key(seed), 9)
    return {
        "tokens": scatter_about(seeds[0], (TOKENS, D), 1.0, 6.0, ((0, 128),)),
        "gain_attn": jnp.clip(1.0 + 0.15 * jax.random.normal(seeds[1], (D,), jnp.float32), 0.25, 1.75),
        "w_qkv": scatter_about(seeds[2], (D, 3, D), D ** -0.5, 0.1875, ((0, 16), (2, 8))),
        "w_out": scatter_about(seeds[3], (D, D), (max(2 * D // LEN, 1)) ** -0.5, 6.0, ((0, 16), (1, 8))),
        "gain_mlp": jnp.clip(1.0 + 0.15 * jax.random.normal(seeds[4], (D,), jnp.float32), 0.25, 1.75),
        "w_in": scatter_about(seeds[5], (D, 2, FF), D ** -0.5, 0.1875, ((0, 16), (2, 8))),
        "w_down": scatter_about(seeds[6], (D, FF), FF ** -0.5, 0.125, ((0, 16), (1, 8))),
        "cotangent": scatter_about(seeds[7], (TOKENS, D), 1.0, 6.0, ((0, 128),)),
    }


@jax.custom_vjp
def low(v):
    return lax.optimization_barrier(v.astype(jnp.bfloat16)).astype(jnp.float32)

@jax.custom_vjp
def low_back(v):
    return v

def low_keep(v):
    return (low(v), None)

def low_pass(kept, grad):
    return (grad,)

def back_keep(v):
    return (v, None)

def back_low(kept, grad):
    return (low(grad),)
low.defvjp(low_keep, low_pass)
low_back.defvjp(back_keep, back_low)
EPSILON = 1e-05
THETA = 160000.0
HIGH = lax.Precision.HIGHEST

def layer_norm(values, gain):
    centre = values - lax.optimization_barrier(jnp.mean(values, axis=-1, keepdims=True))
    scaling = lax.rsqrt(lax.optimization_barrier(jnp.mean(centre * centre, axis=-1, keepdims=True)) + EPSILON)
    return centre * scaling * gain

def rope_tables(length, head_size):
    half = head_size // 2
    freqs = THETA ** (-jnp.arange(half, dtype=jnp.float32) * 2.0 / head_size)
    angles = jnp.arange(length, dtype=jnp.float32)[:, None] * freqs[None, :]
    return (jnp.cos(angles), jnp.sin(angles))

def rotate(values, cosine, sine):
    half = values.shape[-1] // 2
    first = values[..., :half]
    second = values[..., half:]
    cosine = cosine[:, None, :]
    sine = sine[:, None, :]
    return jnp.concatenate([first * cosine - second * sine, second * cosine + first * sine], axis=-1)

def head_attend(item):
    query, key_rows, val_rows = item
    scores = low_back(jnp.einsum('qd,kd->qk', query, key_rows, precision=HIGH) * float(HD) ** (-0.5))
    exponent = jnp.exp(scores - lax.optimization_barrier(jnp.max(scores, axis=1, keepdims=True)))
    probability = exponent / lax.optimization_barrier(jnp.sum(exponent, axis=1, keepdims=True))
    return jnp.einsum('qk,kd->qd', low(probability), val_rows, precision=HIGH)

def forward(resid, gain_attn, w_qkv, w_out, gain_mlp, w_in, w_down):
    normed_attn = low(layer_norm(resid, gain_attn))
    qkv = low_back(jnp.einsum('td,dcj->tcj', normed_attn, w_qkv, precision=HIGH))
    cosine, sine = rope_tables(LEN, HD)
    queries = low(rotate(qkv[:, 0].reshape(LEN, H, HD), cosine, sine))
    keys = low(rotate(qkv[:, 1].reshape(LEN, H, HD), cosine, sine))
    vals = low(qkv[:, 2].reshape(LEN, H, HD))
    mixed = lax.map(jax.checkpoint(head_attend), (queries.transpose(1, 0, 2), keys.transpose(1, 0, 2), vals.transpose(1, 0, 2)))
    mixed = low(low_back(mixed.transpose(1, 0, 2).reshape(LEN, H * HD)))
    attn_sum = low_back(jnp.einsum('tj,ej->te', mixed, w_out, precision=HIGH))
    resid_mid = resid + attn_sum
    normed_mlp = low(layer_norm(resid_mid, gain_mlp))
    hidden_in = low_back(jnp.einsum('td,dcf->tcf', normed_mlp, w_in, precision=HIGH))
    activated = low(jax.nn.gelu(hidden_in[:, 0], approximate=False) * hidden_in[:, 1])
    mlp_sum = low_back(jnp.einsum('tf,ef->te', activated, w_down, precision=HIGH))
    return resid_mid + mlp_sum

def reference(tokens, gain_attn, w_qkv, w_out, gain_mlp, w_in, w_down, cotangent):
    weights = tuple((a.astype(jnp.float32) for a in (gain_attn, w_qkv, w_out, gain_mlp, w_in, w_down)))
    rows = tokens.astype(jnp.float32).reshape(-1, LEN, D)
    backs = cotangent.astype(jnp.float32).reshape(-1, LEN, D)

    def one_seq(carry, item):
        seq_rows, seq_back = item
        result, pull = jax.vjp(forward, seq_rows, *weights)
        grads = pull(seq_back)
        carry = tuple((c + g for c, g in zip(carry, grads[1:])))
        return (carry, (result, grads[0]))
    zero_grads = tuple((jnp.zeros_like(w) for w in weights))
    totals, (results, grad_rows) = lax.scan(one_seq, zero_grads, (rows, backs))
    layer_out = results.reshape(-1, D).astype(jnp.bfloat16)
    grad_tokens = grad_rows.reshape(-1, D).astype(jnp.bfloat16)
    return (layer_out, grad_tokens, totals[0], totals[1], totals[2], totals[3], totals[4], totals[5])
```

```python
import functools

import jax
import jax.numpy as jnp
from jax import lax
from jax.experimental import pallas as pl
from jax.experimental.pallas import tpu as pltpu
from jax.sharding import Mesh
from jax.sharding import PartitionSpec as P

HD = 64
LEN = 1280
EPSILON = 1e-05
THETA = 160000.0
ROWS = 160
WIDTH = 1024
FFB = 328
PAD = 384
QB = 256
VMEM = 60 * 1024 * 1024

AXES = ("x", "zl", "c", "yh", "yl", "zh")
FS = ("x", "zl", "c")
TP = ("yh", "yl", "zh")
MLP_AX = ("yh", "yl")
PRE_AX = ("zh",)
M = 4
PRE = 2
F32 = jnp.float32
BF16 = jnp.bfloat16


def exchange(value, axes, count, mask):
    return lax.ppermute(value, axes, [(i, i ^ mask) for i in range(count)])


def gather_by_mask(value, axes, count):
    return [value] + [exchange(value, axes, count, m) for m in range(1, count)]


def scatter_by_mask(parts, axes, count):
    return [parts[0]] + [exchange(parts[m], axes, count, m) for m in range(1, count)]


def total(parts):
    result = parts[0].astype(F32)
    for part in parts[1:]:
        result = result + part.astype(F32)
    return result


def normalize(values):
    centre = values - jnp.mean(values, axis=-1, keepdims=True)
    scaling = lax.rsqrt(jnp.mean(centre * centre, axis=-1, keepdims=True) + EPSILON)
    return (centre * scaling, scaling)


def norm_back(grad_normed, normed_hat, scaling, gain):
    grad_hat = grad_normed * gain
    mean_grad = jnp.mean(grad_hat, axis=-1, keepdims=True)
    mean_proj = jnp.mean(grad_hat * normed_hat, axis=-1, keepdims=True)
    return (
        scaling * (grad_hat - mean_grad - normed_hat * mean_proj),
        jnp.sum(grad_normed * normed_hat, axis=0),
    )


def rope_tables():
    me = lax.axis_index(TP)
    block = jnp.bitwise_xor(jnp.arange(8, dtype=jnp.int32), me)
    places = (block[:, None] * ROWS + jnp.arange(ROWS, dtype=jnp.int32)[None, :]).reshape(LEN)
    half = HD // 2
    freqs = THETA ** (-jnp.arange(half, dtype=F32) * 2.0 / HD)
    angles = places.astype(F32)[:, None] * freqs[None, :]
    cosine, sine = jnp.cos(angles), jnp.sin(angles)
    return (
        jnp.concatenate([cosine] * 4, axis=1),
        jnp.concatenate([-sine, sine, -sine, sine], axis=1),
    )


def dot(a, b, ca, cb):
    return lax.dot_general(a, b, (((ca,), (cb,)), ((), ())), preferred_element_type=F32)


def swap_halves(values):
    lane = lax.broadcasted_iota(jnp.int32, values.shape, 1)
    first = (lane // 32) % 2 == 0
    return jnp.where(first, pltpu.roll(values, 96, 1), pltpu.roll(values, 32, 1))


def head_mask(values, head):
    lane = lax.broadcasted_iota(jnp.int32, values.shape, 1)
    return jnp.where((lane // HD) == head, values, jnp.zeros_like(values))


def attend_kernel(*refs):
    row_refs = refs[:8]
    w_ref, cos_ref, sin_ref, q_ref, k_ref, v_ref, mixed_ref, lse_ref, rows, proj = refs[8:]
    for r in range(8):
        rows[r * ROWS : (r + 1) * ROWS, :] = row_refs[r][...]
    for c in range(3):
        proj[...] = dot(rows[...], w_ref[c], 1, 0)
        if c == 2:
            v_ref[...] = proj[...].astype(BF16)
        else:
            value = proj[...]
            value = value * cos_ref[...] + swap_halves(value) * sin_ref[...]
            if c == 0:
                q_ref[...] = value.astype(BF16) * jnp.asarray(0.125, BF16)
            else:
                k_ref[...] = value.astype(BF16)

    def block(i, carry):
        at = pl.ds(pl.multiple_of(i * QB, QB), QB)
        query = q_ref[at, :]
        outs = []
        sums = []
        for head in range(2):
            scores = dot(head_mask(query, head), k_ref[...], 1, 1)
            peak = jnp.max(scores, axis=1, keepdims=True)
            exponent = jnp.exp(scores - peak)
            row_sum = jnp.sum(exponent, axis=1, keepdims=True)
            out = dot(exponent.astype(BF16), v_ref[...], 1, 0)
            outs.append(out / row_sum)
            sums.append(jnp.broadcast_to(peak + jnp.log(row_sum), (QB, 2 * HD)))
        lane = lax.broadcasted_iota(jnp.int32, (QB, 2 * HD), 1)
        mixed_ref[at, :] = jnp.where(lane < HD, outs[0], outs[1]).astype(BF16)
        lse_ref[at, :] = jnp.where(lane < HD, sums[0], sums[1])
        return carry

    lax.fori_loop(0, LEN // QB, block, 0)


def attend(row_blocks, w_qkv, cosine, sine):
    wide = jax.ShapeDtypeStruct((LEN, 2 * HD), BF16)
    return pl.pallas_call(
        attend_kernel,
        out_shape=[wide, wide, wide, wide, jax.ShapeDtypeStruct((LEN, 2 * HD), F32)],
        scratch_shapes=[pltpu.VMEM((LEN, WIDTH), BF16), pltpu.VMEM((LEN, 2 * HD), F32)],
        compiler_params=pltpu.CompilerParams(vmem_limit_bytes=VMEM),
        cost_estimate=pl.CostEstimate(
            flops=6_000_000_000, bytes_accessed=8_000_000, transcendentals=3_300_000
        ),
        name="attend",
    )(*row_blocks, w_qkv, cosine, sine)


def attend_back_kernel(
    q_ref, k_ref, v_ref, lse_ref, g_ref, cos_ref, sin_ref, out_ref, key_sum, val_sum
):
    key_sum[...] = jnp.zeros_like(key_sum)
    val_sum[...] = jnp.zeros_like(val_sum)

    def block(i, carry):
        at = pl.ds(pl.multiple_of(i * QB, QB), QB)
        query = q_ref[at, :]
        grad = g_ref[at, :]
        grad_query = jnp.zeros((QB, 2 * HD), F32)
        for head in range(2):
            query_h = head_mask(query, head)
            grad_h = head_mask(grad, head)
            scores = dot(query_h, k_ref[...], 1, 1)
            probs = jnp.exp(scores - lse_ref[at, head * HD : head * HD + 1])
            grad_probs = dot(grad_h, v_ref[...], 1, 1)
            inner = jnp.sum(grad_probs * probs, axis=1, keepdims=True)
            grad_scores = (probs * (grad_probs - inner)).astype(BF16)
            grad_query = grad_query + dot(grad_scores, head_mask(k_ref[...], head), 1, 0)
            key_sum[...] += dot(query_h, grad_scores, 0, 0)
            val_sum[...] += dot(grad_h, probs.astype(BF16), 0, 0)
        grad_query = grad_query * 0.125
        cosine, sine = cos_ref[at, :], sin_ref[at, :]
        out_ref[0, at, :] = (grad_query * cosine - swap_halves(grad_query) * sine).astype(BF16)
        return carry

    lax.fori_loop(0, LEN // QB, block, 0)
    grad_key = key_sum[...].T
    out_ref[1] = (grad_key * cos_ref[...] - swap_halves(grad_key) * sin_ref[...]).astype(BF16)
    out_ref[2] = val_sum[...].T.astype(BF16)


def attend_back(q, k, v, lse, grad_mixed, cosine, sine):
    return pl.pallas_call(
        attend_back_kernel,
        out_shape=jax.ShapeDtypeStruct((3, LEN, 2 * HD), BF16),
        scratch_shapes=[pltpu.VMEM((2 * HD, LEN), F32), pltpu.VMEM((2 * HD, LEN), F32)],
        compiler_params=pltpu.CompilerParams(vmem_limit_bytes=VMEM),
        cost_estimate=pl.CostEstimate(
            flops=12_000_000_000, bytes_accessed=8_000_000, transcendentals=3_300_000
        ),
        name="attend_back",
    )(q, k, v, lse, grad_mixed, cosine, sine)


def mlp_kernel(*refs):
    row_refs, back_refs = refs[:M], refs[M : 2 * M]
    w_ref, act_ref, gh_ref, dn_ref, rows, back, dn = refs[2 * M :]
    step = pl.program_id(0)

    @pl.when(step == 0)
    def _():
        for r in range(M):
            rows[r * ROWS : (r + 1) * ROWS, :] = row_refs[r][...]
            back[r * ROWS : (r + 1) * ROWS, :] = back_refs[r][...]
        dn[...] = jnp.zeros_like(dn)

    w_act = w_ref[:, 0].reshape(WIDTH, PAD)
    w_gate = w_ref[:, 1].reshape(WIDTH, PAD)
    w_down = w_ref[:, 2].reshape(WIDTH, PAD)
    a_in = dot(rows[...], w_act, 1, 0)
    gate = dot(rows[...], w_gate, 1, 0)
    grad_act = dot(back[...], w_down, 1, 0)
    cdf = 0.5 * (1.0 + lax.erf(a_in * (0.5**0.5)))
    gelu = a_in * cdf
    slope = cdf + a_in * (jnp.exp(-0.5 * a_in * a_in) * 0.3989422804014327)
    act_ref[0] = (gelu * gate).astype(BF16)
    g_act = (grad_act * gate * slope).astype(BF16)
    g_gate = (grad_act * gelu).astype(BF16)
    gh_ref[0, 0] = g_act
    gh_ref[0, 1] = g_gate
    dn[...] += dot(g_act, w_act, 1, 1) + dot(g_gate, w_gate, 1, 1)

    @pl.when(step == PRE - 1)
    def _():
        for r in range(M):
            dn_ref[r] = dn[r * ROWS : (r + 1) * ROWS, :].astype(BF16)


def mlp(row_blocks, back_blocks, weights):
    group = M * ROWS
    whole = pl.BlockSpec((ROWS, WIDTH), lambda p: (0, 0))
    return pl.pallas_call(
        mlp_kernel,
        grid=(PRE,),
        in_specs=[whole] * (2 * M) + [pl.BlockSpec((16, 3, 64, PAD), lambda p: (0, p, 0, 0))],
        out_specs=[
            pl.BlockSpec((1, group, PAD), lambda p: (p, 0, 0)),
            pl.BlockSpec((1, 2, group, PAD), lambda p: (p, 0, 0, 0)),
            pl.BlockSpec((M, ROWS, WIDTH), lambda p: (0, 0, 0)),
        ],
        out_shape=[
            jax.ShapeDtypeStruct((PRE, group, PAD), BF16),
            jax.ShapeDtypeStruct((PRE, 2, group, PAD), BF16),
            jax.ShapeDtypeStruct((M, ROWS, WIDTH), BF16),
        ],
        scratch_shapes=[
            pltpu.VMEM((group, WIDTH), BF16),
            pltpu.VMEM((group, WIDTH), BF16),
            pltpu.VMEM((group, WIDTH), F32),
        ],
        compiler_params=pltpu.CompilerParams(vmem_limit_bytes=VMEM),
        cost_estimate=pl.CostEstimate(
            flops=10_000_000_000, bytes_accessed=10_000_000, transcendentals=1_000_000
        ),
        name="mlp",
    )(*row_blocks, *back_blocks, weights)


def mlp_grads_kernel(*refs):
    row_refs, back_refs = refs[:M], refs[M : 2 * M]
    w_ref, act_ref, gh_ref, grad_ref, sum_ref, rows, back, sums = refs[2 * M :]
    step = pl.program_id(0)

    @pl.when(step == 0)
    def _():
        for r in range(M):
            rows[:, r * ROWS : (r + 1) * ROWS] = row_refs[r][...].T
            back[:, r * ROWS : (r + 1) * ROWS] = back_refs[r][...].T
        sums[...] = jnp.zeros_like(sums)

    grad_ref[:, 0] = dot(rows[...], gh_ref[0, 0], 1, 0).astype(BF16).reshape(16, 64, PAD)
    grad_ref[:, 1] = dot(rows[...], gh_ref[0, 1], 1, 0).astype(BF16).reshape(16, 64, PAD)
    grad_ref[:, 2] = dot(back[...], act_ref[0], 1, 0).astype(BF16).reshape(16, 64, PAD)
    sums[...] += dot(act_ref[0], w_ref[:, 0].reshape(WIDTH, PAD), 1, 1)

    @pl.when(step == PRE - 1)
    def _():
        for r in range(M):
            sum_ref[r] = sums[r * ROWS : (r + 1) * ROWS, :].astype(BF16)


def mlp_grads(row_blocks, back_blocks, weights, act, grad_hidden):
    group = M * ROWS
    whole = pl.BlockSpec((ROWS, WIDTH), lambda p: (0, 0))
    return pl.pallas_call(
        mlp_grads_kernel,
        grid=(PRE,),
        in_specs=[whole] * (2 * M)
        + [
            pl.BlockSpec((16, 1, 64, PAD), lambda p: (0, 3 * p + 2, 0, 0)),
            pl.BlockSpec((1, group, PAD), lambda p: (p, 0, 0)),
            pl.BlockSpec((1, 2, group, PAD), lambda p: (p, 0, 0, 0)),
        ],
        out_specs=[
            pl.BlockSpec((16, 3, 64, PAD), lambda p: (0, p, 0, 0)),
            pl.BlockSpec((M, ROWS, WIDTH), lambda p: (0, 0, 0)),
        ],
        out_shape=[
            jax.ShapeDtypeStruct((16, 3 * PRE, 64, PAD), BF16),
            jax.ShapeDtypeStruct((M, ROWS, WIDTH), BF16),
        ],
        scratch_shapes=[
            pltpu.VMEM((WIDTH, group), BF16),
            pltpu.VMEM((WIDTH, group), BF16),
            pltpu.VMEM((group, WIDTH), F32),
        ],
        compiler_params=pltpu.CompilerParams(vmem_limit_bytes=VMEM),
        cost_estimate=pl.CostEstimate(
            flops=8_000_000_000, bytes_accessed=12_000_000, transcendentals=0
        ),
        name="mlp_grads",
    )(*row_blocks, *back_blocks, weights, act, grad_hidden)


def halve(value, axis, axes_count_mask):
    bit = lax.axis_index(axis)
    size = value.shape[0] // 2
    keep = lax.dynamic_slice_in_dim(value, bit * size, size, 0)
    send = lax.dynamic_slice_in_dim(value, (1 - bit) * size, size, 0)
    got = lax.ppermute(send, axis, [(0, 1), (1, 0)])
    return keep.astype(F32) + got.astype(F32)


def reduce_over_fsdp(partial):
    width = partial.shape[1]
    array = partial.reshape(4, 2, 2, 64, width).transpose(2, 1, 0, 3, 4)
    array = halve(array, "c", 2)[0]
    array = halve(array.astype(BF16), "zl", 2)[0]
    array = array.astype(BF16)
    me = lax.axis_index("x")
    parts = [
        lax.dynamic_index_in_dim(array, jnp.bitwise_xor(me, m), 0, keepdims=False)
        for m in range(4)
    ]
    return total(scatter_by_mask(parts, ("x",), 4))


def on_device(tokens, gain_attn, w_qkv, w_out, gain_mlp, w_in, w_down, cotangent):
    mlp_shard = jnp.concatenate([w_in, w_down[:, None, :]], axis=1).transpose(1, 0, 2)
    mlp_shard = jnp.pad(mlp_shard, ((0, 0), (0, 0), (0, PAD - FFB)))
    mlp_shards = gather_by_mask(mlp_shard, PRE_AX, PRE)
    out_shards = gather_by_mask(w_out, TP, 8)
    out_wide = jnp.concatenate(out_shards + [jnp.zeros_like(w_out)], axis=1)
    out_wide = out_wide.reshape(64, 3, PAD).transpose(1, 0, 2)
    shards = jnp.concatenate(mlp_shards + [out_wide], axis=0)
    weights = lax.all_gather(shards, FS, axis=0, tiled=False)
    full_qkv = lax.all_gather(w_qkv.transpose(1, 0, 2), FS, axis=1, tiled=True)
    cosine, sine = rope_tables()

    resid = tokens.astype(F32)
    hat_attn, scale_attn = normalize(resid)
    normed_attn = (hat_attn * gain_attn).astype(BF16)
    rows_attn = gather_by_mask(normed_attn, TP, 8)
    q, k, v, mixed, lse = attend(rows_attn, full_qkv, cosine, sine)
    mixed_parts = scatter_by_mask(list(mixed.reshape(8, ROWS, 2 * HD)), TP, 8)
    mixed_own = jnp.concatenate(mixed_parts, axis=1)
    full_out = [weights[:, 3 * PRE + b].reshape(WIDTH, PAD) for b in range(3)]
    full_out = jnp.concatenate(full_out, axis=1)[:, :WIDTH]
    attn_sum = dot(mixed_own, full_out, 1, 1)
    resid_mid = resid + attn_sum
    hat_mlp, scale_mlp = normalize(resid_mid)
    normed_mlp = (hat_mlp * gain_mlp).astype(BF16)

    back_blocks = gather_by_mask(cotangent, MLP_AX, M)
    row_blocks = gather_by_mask(normed_mlp, MLP_AX, M)
    act, grad_hidden, dn_parts = mlp(row_blocks, back_blocks, weights)
    grad_normed_mlp = total(scatter_by_mask(list(dn_parts), MLP_AX, M))
    grads, sum_parts = mlp_grads(row_blocks, back_blocks, weights, act, grad_hidden)
    grads = lax.psum_scatter(grads, FS, scatter_dimension=0, tiled=False)
    mlp_sum = total(scatter_by_mask(list(sum_parts), MLP_AX, M))
    layer_out = (resid_mid + mlp_sum).astype(BF16)

    grad_mid_norm, gain_mlp_part = norm_back(grad_normed_mlp, hat_mlp, scale_mlp, gain_mlp)
    grad_mid = cotangent.astype(F32) + grad_mid_norm
    grad_attn = grad_mid.astype(BF16)
    grad_mixed = dot(grad_attn, full_out, 1, 0).astype(BF16)
    grad_out = dot(grad_attn, mixed_own, 0, 0).astype(BF16)
    gm_parts = [grad_mixed[:, 2 * HD * m : 2 * HD * (m + 1)] for m in range(8)]
    gm_own = jnp.concatenate(scatter_by_mask(gm_parts, TP, 8), axis=0)
    grad_qkv = attend_back(q, k, v, lse, gm_own, cosine, sine)

    dn_attn = sum(dot(grad_qkv[c], full_qkv[c], 1, 1) for c in range(3)).astype(BF16)
    dn_attn_parts = list(dn_attn.reshape(8, ROWS, WIDTH))
    grad_normed_attn = total(scatter_by_mask(dn_attn_parts, TP, 8))
    rows_all = jnp.concatenate(rows_attn, axis=0)
    grad_qkv_w = jnp.concatenate([dot(rows_all, grad_qkv[c], 0, 0) for c in range(3)], axis=1)

    grad_out = reduce_over_fsdp(grad_out).astype(BF16)
    grad_out = total(
        scatter_by_mask([grad_out[:, 2 * HD * m : 2 * HD * (m + 1)] for m in range(8)], TP, 8)
    )
    grad_qkv_w = reduce_over_fsdp(grad_qkv_w.astype(BF16)).reshape(64, 3, 2 * HD)

    grad_parts = [grads[3 * p : 3 * p + 3] for p in range(PRE)]
    grad_mlp = total(scatter_by_mask(grad_parts, PRE_AX, PRE))
    grad_in = grad_mlp[:2, :, :FFB].transpose(1, 0, 2)
    grad_down = grad_mlp[2, :, :FFB]

    grad_first, gain_attn_part = norm_back(grad_normed_attn, hat_attn, scale_attn, gain_attn)
    grad_tokens = (grad_mid + grad_first).astype(BF16)
    gains = jnp.stack([gain_attn_part, gain_mlp_part])
    for axis in AXES:
        if axis == "x":
            gains = gains + lax.ppermute(gains, "x", [(0, 1), (1, 0), (2, 3), (3, 2)])
            gains = gains + lax.ppermute(gains, "x", [(0, 3), (1, 2), (2, 1), (3, 0)])
        else:
            gains = gains + lax.ppermute(gains, axis, [(0, 1), (1, 0)])
    return (
        layer_out,
        grad_tokens,
        gains[0],
        grad_qkv_w,
        grad_out,
        gains[1],
        grad_in,
        grad_down,
    )


def solution(mesh):
    fine = Mesh(mesh.devices.reshape(4, 2, 2, 2, 2, 2), AXES)
    in_specs = (
        P(AXES, None),
        P(),
        P(FS, None, TP),
        P(FS, TP),
        P(),
        P(FS, None, TP),
        P(FS, TP),
        P(AXES, None),
    )
    out_specs = (
        P(AXES, None),
        P(AXES, None),
        P(),
        P(FS, None, TP),
        P(FS, TP),
        P(),
        P(FS, None, TP),
        P(FS, TP),
    )
    return jax.shard_map(
        on_device, mesh=fine, in_specs=in_specs, out_specs=out_specs, check_vma=False
    )
```

```python
import jax
import jax.numpy as jnp
from jax import lax
from jax.experimental import pallas as pl
from jax.experimental.pallas import tpu as pltpu
from jax.sharding import Mesh
from jax.sharding import PartitionSpec as P

HD = 64
LEN = 1280
EPSILON = 1e-05
THETA = 160000.0
ROWS = 160
WIDTH = 1024
FFB = 328
PAD = 384
QB = 256
SENT = 176
VMEM = 60 * 1024 * 1024

AXES = ("x", "zl", "c", "yh", "yl", "zh")
FS = ("x", "zl", "c")
TP = ("yh", "yl", "zh")
MLP_AX = ("yh", "yl")
PRE_AX = ("zh",)
M = 4
PRE = 2
F32 = jnp.float32
BF16 = jnp.bfloat16


def exchange(value, axes, count, mask):
    return lax.ppermute(value, axes, [(i, i ^ mask) for i in range(count)])


def gather_by_mask(value, axes, count):
    return [value] + [exchange(value, axes, count, m) for m in range(1, count)]


def scatter_by_mask(parts, axes, count):
    return [parts[0]] + [exchange(parts[m], axes, count, m) for m in range(1, count)]


def total(parts):
    result = parts[0].astype(F32)
    for part in parts[1:]:
        result = result + part.astype(F32)
    return result


def normalize(values):
    centre = values - jnp.mean(values, axis=-1, keepdims=True)
    scaling = lax.rsqrt(jnp.mean(centre * centre, axis=-1, keepdims=True) + EPSILON)
    return (centre * scaling, scaling)


def norm_back(grad_normed, normed_hat, scaling, gain):
    grad_hat = grad_normed * gain
    mean_grad = jnp.mean(grad_hat, axis=-1, keepdims=True)
    mean_proj = jnp.mean(grad_hat * normed_hat, axis=-1, keepdims=True)
    return (
        scaling * (grad_hat - mean_grad - normed_hat * mean_proj),
        jnp.sum(grad_normed * normed_hat, axis=0),
    )


def rope_tables():
    half = HD // 2
    freqs = THETA ** (-jnp.arange(half, dtype=F32) * 2.0 / HD)
    angles = jnp.arange(LEN, dtype=F32)[:, None] * freqs[None, :]
    cosine, sine = jnp.cos(angles), jnp.sin(angles)
    return (
        jnp.concatenate([cosine] * 4, axis=1),
        jnp.concatenate([-sine, sine, -sine, sine], axis=1),
    )


def dot(a, b, ca, cb):
    return lax.dot_general(a, b, (((ca,), (cb,)), ((), ())), preferred_element_type=F32)


def swap_halves(values):
    lane = lax.broadcasted_iota(jnp.int32, values.shape, 1)
    first = (lane // 32) % 2 == 0
    return jnp.where(first, pltpu.roll(values, 96, 1), pltpu.roll(values, 32, 1))


def head_mask(values, head):
    lane = lax.broadcasted_iota(jnp.int32, values.shape, 1)
    return jnp.where((lane // HD) == head, values, jnp.zeros_like(values))


def attend_kernel(
    rows_ref, w_ref, cos_ref, sin_ref, q_ref, k_ref, v_ref, mixed_ref, lse_ref, proj
):
    proj[...] = dot(rows_ref[...].reshape(LEN, WIDTH), w_ref[...].reshape(WIDTH, PAD), 1, 0)
    cosine, sine = cos_ref[...], sin_ref[...]
    value = proj[:, : 2 * HD]
    value = value * cosine + swap_halves(value) * sine
    q_ref[...] = value.astype(BF16) * jnp.asarray(0.125, BF16)
    value = proj[:, 2 * HD : 4 * HD]
    k_ref[...] = (value * cosine + swap_halves(value) * sine).astype(BF16)
    v_ref[...] = proj[:, 4 * HD :].astype(BF16)

    def block(i, carry):
        at = pl.ds(pl.multiple_of(i * QB, QB), QB)
        query = q_ref[at, :]
        outs = []
        sums = []
        for head in range(2):
            scores = dot(head_mask(query, head), k_ref[...], 1, 1)
            peak = jnp.max(scores, axis=1, keepdims=True)
            exponent = jnp.exp(scores - peak)
            row_sum = jnp.sum(exponent, axis=1, keepdims=True)
            out = dot(exponent.astype(BF16), v_ref[...], 1, 0)
            outs.append(out / row_sum)
            sums.append(jnp.broadcast_to(peak + jnp.log(row_sum), (QB, 2 * HD)))
        lane = lax.broadcasted_iota(jnp.int32, (QB, 2 * HD), 1)
        mixed_ref[at, :] = jnp.where(lane < HD, outs[0], outs[1]).astype(BF16)
        lse_ref[at, :] = jnp.where(lane < HD, sums[0], sums[1])
        return carry

    lax.fori_loop(0, LEN // QB, block, 0)


def whole(*shape):
    return pl.BlockSpec(shape, lambda i: (0,) * len(shape))


ROWS_SPEC = pl.BlockSpec((8, ROWS, WIDTH), lambda i: (0, 0, 0))
QKV_SPEC = pl.BlockSpec((16, 1, 64, PAD), lambda i: (0, 3, 0, 0))


def attend(rows, weights, cosine, sine):
    wide = jax.ShapeDtypeStruct((LEN, 2 * HD), BF16)
    return pl.pallas_call(
        attend_kernel,
        grid=(1,),
        in_specs=[ROWS_SPEC, QKV_SPEC, whole(LEN, 2 * HD), whole(LEN, 2 * HD)],
        out_specs=[whole(LEN, 2 * HD)] * 5,
        out_shape=[wide, wide, wide, wide, jax.ShapeDtypeStruct((LEN, 2 * HD), F32)],
        scratch_shapes=[pltpu.VMEM((LEN, PAD), F32)],
        compiler_params=pltpu.CompilerParams(vmem_limit_bytes=VMEM),
        cost_estimate=pl.CostEstimate(
            flops=6_000_000_000, bytes_accessed=8_000_000, transcendentals=3_300_000
        ),
        name="attend",
    )(rows, weights, cosine, sine)


def attend_back_kernel(me_ref, *refs):
    q_ref, k_ref, v_ref, lse_ref, g_ref, cos_ref, sin_ref, w_ref, out_ref = refs[:9]
    dn_refs = refs[9:17]
    key_sum, val_sum, dn = refs[17:]
    key_sum[...] = jnp.zeros_like(key_sum)
    val_sum[...] = jnp.zeros_like(val_sum)

    def block(i, carry):
        at = pl.ds(pl.multiple_of(i * QB, QB), QB)
        query = q_ref[at, :]
        grad = g_ref[at, :]
        grad_query = jnp.zeros((QB, 2 * HD), F32)
        for head in range(2):
            query_h = head_mask(query, head)
            grad_h = head_mask(grad, head)
            scores = dot(query_h, k_ref[...], 1, 1)
            probs = jnp.exp(scores - lse_ref[at, head * HD : head * HD + 1])
            grad_probs = dot(grad_h, v_ref[...], 1, 1)
            inner = jnp.sum(grad_probs * probs, axis=1, keepdims=True)
            grad_scores = (probs * (grad_probs - inner)).astype(BF16)
            grad_query = grad_query + dot(grad_scores, head_mask(k_ref[...], head), 1, 0)
            key_sum[...] += dot(query_h, grad_scores, 0, 0)
            val_sum[...] += dot(grad_h, probs.astype(BF16), 0, 0)
        grad_query = grad_query * 0.125
        cosine, sine = cos_ref[at, :], sin_ref[at, :]
        grad_query = grad_query * cosine - swap_halves(grad_query) * sine
        out_ref[at, : 2 * HD] = grad_query.astype(BF16)
        return carry

    lax.fori_loop(0, LEN // QB, block, 0)
    grad_key = key_sum[...].T
    grad_key = grad_key * cos_ref[...] - swap_halves(grad_key) * sin_ref[...]
    out_ref[:, 2 * HD : 4 * HD] = grad_key.astype(BF16)
    out_ref[:, 4 * HD :] = val_sum[...].T.astype(BF16)
    dn[...] = dot(out_ref[...], w_ref[...].reshape(WIDTH, PAD), 1, 1).astype(BF16)
    me = me_ref[0]
    for m in range(8):
        at = pl.multiple_of(jnp.bitwise_xor(me, m) * ROWS, ROWS)
        dn_refs[m][...] = dn[pl.ds(at, ROWS), :]


def attend_back(me, q, k, v, lse, grad_mixed, cosine, sine, weights):
    return pl.pallas_call(
        attend_back_kernel,
        grid=(1,),
        in_specs=[pl.BlockSpec(memory_space=pltpu.SMEM)]
        + [whole(LEN, 2 * HD)] * 7
        + [QKV_SPEC],
        out_specs=[whole(LEN, PAD)] + [whole(ROWS, WIDTH)] * 8,
        out_shape=[jax.ShapeDtypeStruct((LEN, PAD), BF16)]
        + [jax.ShapeDtypeStruct((ROWS, WIDTH), BF16)] * 8,
        scratch_shapes=[
            pltpu.VMEM((2 * HD, LEN), F32),
            pltpu.VMEM((2 * HD, LEN), F32),
            pltpu.VMEM((LEN, WIDTH), BF16),
        ],
        compiler_params=pltpu.CompilerParams(vmem_limit_bytes=VMEM),
        cost_estimate=pl.CostEstimate(
            flops=12_000_000_000, bytes_accessed=8_000_000, transcendentals=3_300_000
        ),
        name="attend_back",
    )(me, q, k, v, lse, grad_mixed, cosine, sine, weights)


def qkv_grads_kernel(rows_ref, g_ref, out_ref, turned):
    for r in range(8):
        turned[:, r * ROWS : (r + 1) * ROWS] = rows_ref[r].T
    out_ref[...] = dot(turned[...], g_ref[...], 1, 0).astype(BF16).reshape(16, 64, PAD)


def qkv_grads(rows, grad_qkv):
    return pl.pallas_call(
        qkv_grads_kernel,
        grid=(1,),
        in_specs=[ROWS_SPEC, whole(LEN, PAD)],
        out_specs=whole(16, 64, PAD),
        out_shape=jax.ShapeDtypeStruct((16, 64, PAD), BF16),
        scratch_shapes=[pltpu.VMEM((WIDTH, LEN), BF16)],
        compiler_params=pltpu.CompilerParams(vmem_limit_bytes=VMEM),
        cost_estimate=pl.CostEstimate(
            flops=2_000_000_000, bytes_accessed=5_000_000, transcendentals=0
        ),
        name="qkv_grads",
    )(rows, grad_qkv)


def store_by_owner(ref, at, value):
    value = value.astype(BF16)
    for x in range(4):
        for zl in range(2):
            for c in range(2):
                row = (x * 4 + zl * 2 + c) * 64
                ref[x * 2 + c, zl, at] = value[row : row + 64, :]


def mlp_kernel(*refs):
    row_refs, back_refs = refs[:M], refs[M : 2 * M]
    w0_ref, w1_ref, act_ref, gh_ref = refs[2 * M : 2 * M + 4]
    dn_refs = refs[2 * M + 4 : 3 * M + 4]
    rows, back, dn, weights = refs[3 * M + 4 :]
    step = pl.program_id(0)

    @pl.when(step == 0)
    def _():
        for r in range(M):
            rows[r * ROWS : (r + 1) * ROWS, :] = row_refs[r][...]
            back[r * ROWS : (r + 1) * ROWS, :] = back_refs[r][...]
        dn[...] = jnp.zeros_like(dn)
        weights[...] = w0_ref[...]

    @pl.when(step == 1)
    def _():
        weights[...] = w1_ref[...]

    w_act = weights[:, 0].reshape(WIDTH, PAD)
    w_gate = weights[:, 1].reshape(WIDTH, PAD)
    w_down = weights[:, 2].reshape(WIDTH, PAD)
    a_in = dot(rows[...], w_act, 1, 0)
    gate = dot(rows[...], w_gate, 1, 0)
    grad_act = dot(back[...], w_down, 1, 0)
    cdf = 0.5 * (1.0 + lax.erf(a_in * (0.5**0.5)))
    gelu = a_in * cdf
    slope = cdf + a_in * (jnp.exp(-0.5 * a_in * a_in) * 0.3989422804014327)
    act_ref[0] = (gelu * gate).astype(BF16)
    g_act = (grad_act * gate * slope).astype(BF16)
    g_gate = (grad_act * gelu).astype(BF16)
    gh_ref[0, 0] = g_act
    gh_ref[0, 1] = g_gate
    dn[...] += dot(g_act, w_act, 1, 1) + dot(g_gate, w_gate, 1, 1)

    @pl.when(step == PRE - 1)
    def _():
        for r in range(M):
            dn_refs[r][...] = dn[r * ROWS : (r + 1) * ROWS, :].astype(BF16)


MLP_SPEC = pl.BlockSpec((16, 3, 64, PAD), lambda p: (0, 0, 0, 0))
DOWN_SPEC = pl.BlockSpec((16, 1, 64, PAD), lambda p: (0, 2, 0, 0))
ACT_SPEC = pl.BlockSpec((1, M * ROWS, PAD), lambda p: (p, 0, 0))
HIDDEN_SPEC = pl.BlockSpec((1, 2, M * ROWS, PAD), lambda p: (p, 0, 0, 0))


def mlp(row_blocks, back_blocks, weights, weights_more):
    group = M * ROWS
    return pl.pallas_call(
        mlp_kernel,
        grid=(PRE,),
        in_specs=[whole(ROWS, WIDTH)] * (2 * M) + [MLP_SPEC, MLP_SPEC],
        out_specs=[ACT_SPEC, HIDDEN_SPEC] + [whole(ROWS, WIDTH)] * M,
        out_shape=[
            jax.ShapeDtypeStruct((PRE, group, PAD), BF16),
            jax.ShapeDtypeStruct((PRE, 2, group, PAD), BF16),
        ]
        + [jax.ShapeDtypeStruct((ROWS, WIDTH), BF16)] * M,
        scratch_shapes=[
            pltpu.VMEM((group, WIDTH), BF16),
            pltpu.VMEM((group, WIDTH), BF16),
            pltpu.VMEM((group, WIDTH), F32),
            pltpu.VMEM((16, 3, 64, PAD), BF16),
        ],
        compiler_params=pltpu.CompilerParams(vmem_limit_bytes=VMEM),
        cost_estimate=pl.CostEstimate(
            flops=10_000_000_000, bytes_accessed=10_000_000, transcendentals=1_000_000
        ),
        name="mlp",
    )(*row_blocks, *back_blocks, weights, weights_more)


def mlp_grads_kernel(*refs):
    row_refs, back_refs = refs[:M], refs[M : 2 * M]
    w0_ref, w1_ref, act_ref, gh_ref, grad_ref = refs[2 * M : 2 * M + 5]
    sum_refs = refs[2 * M + 5 : 3 * M + 5]
    rows, back, sums = refs[3 * M + 5 :]
    step = pl.program_id(0)

    @pl.when(step == 0)
    def _():
        for r in range(M):
            rows[:, r * ROWS : (r + 1) * ROWS] = row_refs[r][...].T
            back[:, r * ROWS : (r + 1) * ROWS] = back_refs[r][...].T
        sums[...] = dot(act_ref[0], w0_ref[...].reshape(WIDTH, PAD), 1, 1)

    store_by_owner(grad_ref, 0, dot(rows[...], gh_ref[0, 0], 1, 0))
    store_by_owner(grad_ref, 1, dot(rows[...], gh_ref[0, 1], 1, 0))
    store_by_owner(grad_ref, 2, dot(back[...], act_ref[0], 1, 0))

    @pl.when(step == 1)
    def _():
        sums[...] += dot(act_ref[0], w1_ref[...].reshape(WIDTH, PAD), 1, 1)
        for r in range(M):
            sum_refs[r][...] = sums[r * ROWS : (r + 1) * ROWS, :].astype(BF16)


def mlp_grads(row_blocks, back_blocks, weights, weights_more, act, grad_hidden):
    group = M * ROWS
    return pl.pallas_call(
        mlp_grads_kernel,
        grid=(PRE,),
        in_specs=[whole(ROWS, WIDTH)] * (2 * M)
        + [DOWN_SPEC, DOWN_SPEC, ACT_SPEC, HIDDEN_SPEC],
        out_specs=[pl.BlockSpec((8, 2, 3, 64, PAD), lambda p: (0, 0, p, 0, 0))]
        + [whole(ROWS, WIDTH)] * M,
        out_shape=[jax.ShapeDtypeStruct((8, 2, 3 * PRE + 3, 64, PAD), BF16)]
        + [jax.ShapeDtypeStruct((ROWS, WIDTH), BF16)] * M,
        scratch_shapes=[
            pltpu.VMEM((WIDTH, group), BF16),
            pltpu.VMEM((WIDTH, group), BF16),
            pltpu.VMEM((group, WIDTH), F32),
        ],
        compiler_params=pltpu.CompilerParams(vmem_limit_bytes=VMEM),
        cost_estimate=pl.CostEstimate(
            flops=8_000_000_000, bytes_accessed=12_000_000, transcendentals=0
        ),
        name="mlp_grads",
    )(*row_blocks, *back_blocks, weights, weights_more, act, grad_hidden)


def out_grads_kernel(g_ref, mixed_ref, held_ref, grad_ref):
    del held_ref
    turned = g_ref[...].T
    for b in range(3):
        columns = mixed_ref[:, b * PAD : (b + 1) * PAD]
        store_by_owner(grad_ref, b, dot(turned, columns, 1, 0))


def out_grads(grad_attn, mixed_own, grads):
    return pl.pallas_call(
        out_grads_kernel,
        grid=(1,),
        in_specs=[whole(ROWS, WIDTH), whole(ROWS, 3 * PAD), pl.BlockSpec(memory_space=pl.ANY)],
        out_specs=pl.BlockSpec((8, 2, 3, 64, PAD), lambda p: (0, 0, PRE, 0, 0)),
        out_shape=jax.ShapeDtypeStruct(grads.shape, BF16),
        input_output_aliases={2: 0},
        compiler_params=pltpu.CompilerParams(vmem_limit_bytes=VMEM),
        cost_estimate=pl.CostEstimate(
            flops=400_000_000, bytes_accessed=4_000_000, transcendentals=0
        ),
        name="out_grads",
    )(grad_attn, mixed_own, grads)


def two_parts(value):
    high = value.astype(BF16)
    return high, (value - high.astype(F32)).astype(BF16)


def on_device(tokens, gain_attn, w_qkv, w_out, gain_mlp, w_in, w_down, cotangent):
    own_mlp = jnp.concatenate([w_in, w_down[:, None, :]], axis=1).transpose(1, 0, 2)
    own_mlp = jnp.pad(own_mlp, ((0, 0), (0, 0), (0, PAD - FFB)))
    own_qkv = w_qkv.reshape(64, PAD)
    weights = lax.all_gather(jnp.concatenate([own_mlp, own_qkv[None]], axis=0), FS, axis=0)
    partner_mlp = exchange(own_mlp, PRE_AX, PRE, 1)
    cosine, sine = rope_tables()

    resid = tokens.astype(F32)
    hat_attn, scale_attn = normalize(resid)
    normed_attn = (hat_attn * gain_attn).astype(BF16)
    sent = jnp.concatenate(
        [normed_attn, w_out.reshape(8, WIDTH), jnp.zeros((SENT - ROWS - 8, WIDTH), BF16)], axis=0
    )
    sent = jnp.broadcast_to(sent[None], (8, SENT, WIDTH))
    rows = lax.all_to_all(sent, TP, 0, 0)
    out_wide = rows[:, ROWS : ROWS + 8].reshape(8, 64, 2 * HD).transpose(1, 0, 2)
    out_wide = jnp.pad(out_wide.reshape(64, WIDTH), ((0, 0), (0, 3 * PAD - WIDTH)))
    out_wide = out_wide.reshape(64, 3, PAD).transpose(1, 0, 2)
    weights_more = lax.all_gather(jnp.concatenate([partner_mlp, out_wide], axis=0), FS, axis=0)

    cotangent_later, rows = lax.optimization_barrier((cotangent, rows))
    back_blocks = gather_by_mask(cotangent_later, MLP_AX, M)
    q, k, v, mixed, lse = attend(rows, weights, cosine, sine)
    mixed_own = lax.all_to_all(mixed.reshape(8, ROWS, 2 * HD), TP, 0, 0)
    mixed_own = mixed_own.transpose(1, 0, 2).reshape(ROWS, WIDTH)
    mixed_own = jnp.pad(mixed_own, ((0, 0), (0, 3 * PAD - WIDTH)))
    full_out = [weights_more[:, 3 + b].reshape(WIDTH, PAD) for b in range(3)]
    attn_sum = sum(
        dot(mixed_own[:, b * PAD : (b + 1) * PAD], full_out[b], 1, 1) for b in range(3)
    )
    resid_mid = resid + attn_sum
    hat_mlp, scale_mlp = normalize(resid_mid)
    normed_mlp = (hat_mlp * gain_mlp).astype(BF16)

    row_blocks = gather_by_mask(normed_mlp, MLP_AX, M)
    act, grad_hidden, *dn_parts = mlp(row_blocks, back_blocks, weights, weights_more)
    grad_normed_mlp = total(scatter_by_mask(dn_parts, MLP_AX, M))
    grads, *sum_parts = mlp_grads(
        row_blocks, back_blocks, weights, weights_more, act, grad_hidden
    )

    grad_mid_norm, gain_mlp_part = norm_back(grad_normed_mlp, hat_mlp, scale_mlp, gain_mlp)
    grad_mid = cotangent.astype(F32) + grad_mid_norm
    grad_attn = grad_mid.astype(BF16)
    grad_mixed = jnp.concatenate([dot(grad_attn, full_out[b], 1, 0) for b in range(3)], axis=1)
    grad_mixed = grad_mixed[:, :WIDTH].astype(BF16)
    gm_parts = grad_mixed.reshape(ROWS, 8, 2 * HD).transpose(1, 0, 2)
    grads = out_grads(grad_attn, mixed_own, grads)
    gm_parts, grads = lax.optimization_barrier((gm_parts, grads))
    grads = lax.psum_scatter(grads, ("x", "c"), scatter_dimension=0)
    gm_own = lax.all_to_all(gm_parts, TP, 0, 0).reshape(LEN, 2 * HD)

    *sum_parts, gm_own = lax.optimization_barrier((*sum_parts, gm_own))
    mlp_sum = total(scatter_by_mask(sum_parts, MLP_AX, M))
    layer_out = (resid_mid + mlp_sum).astype(BF16)
    me = lax.axis_index(TP).astype(jnp.int32)[None]
    grad_qkv, *dn_attn_parts = attend_back(
        me, q, k, v, lse, gm_own, cosine, sine, weights
    )
    grad_normed_attn = total(scatter_by_mask(dn_attn_parts, TP, 8))

    qkv_part = qkv_grads(rows, grad_qkv)
    high, low = two_parts(gain_mlp_part.reshape(16, 1, 64))
    extra = jnp.pad(jnp.concatenate([high, low], axis=1), ((0, 0), (0, 14), (0, PAD - 64)))
    got = lax.all_to_all(jnp.concatenate([qkv_part, extra], axis=1), FS, 0, 0)
    got = jnp.sum(got.astype(F32), axis=0)
    grad_qkv_w = got[:64]
    gain_mlp_own = got[64, :64] + got[65, :64]
    gain_own = lax.dynamic_slice_in_dim(gain_attn, lax.axis_index(FS) * 64, 64)
    gain_attn_own = jnp.sum(grad_qkv_w * own_qkv.astype(F32), axis=1) / gain_own
    gains = jnp.concatenate([gain_attn_own, gain_mlp_own])
    gains = jnp.broadcast_to(gains[None, None], (128, 1, 128))
    gains = lax.all_to_all(gains, AXES, 0, 0).reshape(16, 8, 128).sum(axis=1)

    bit = lax.axis_index("zl")
    keep = lax.dynamic_index_in_dim(grads, bit, 0, keepdims=False)
    send = lax.dynamic_index_in_dim(grads, 1 - bit, 0, keepdims=False)
    halves = keep.astype(F32) + exchange(send, ("zl",), 2, 1).astype(F32)
    from_partner = exchange(halves[3:6].astype(BF16), PRE_AX, PRE, 1)
    grad_mlp = halves[:3] + from_partner.astype(F32)
    grad_in = grad_mlp[:2, :, :FFB].transpose(1, 0, 2)
    grad_down = grad_mlp[2, :, :FFB]
    out_parts = halves[6:].astype(BF16).transpose(1, 0, 2).reshape(64, 3 * PAD)[:, :WIDTH]
    out_parts = out_parts.reshape(64, 8, 2 * HD).transpose(1, 0, 2)
    grad_out = jnp.sum(lax.all_to_all(out_parts, TP, 0, 0).astype(F32), axis=0)

    grad_first, _ = norm_back(grad_normed_attn, hat_attn, scale_attn, gain_attn)
    grad_tokens = (grad_mid + grad_first).astype(BF16)
    return (
        layer_out,
        grad_tokens,
        gains[:, :64].reshape(WIDTH),
        grad_qkv_w.reshape(64, 3, 2 * HD),
        grad_out,
        gains[:, 64:].reshape(WIDTH),
        grad_in,
        grad_down,
    )


def solution(mesh):
    fine = Mesh(mesh.devices.reshape(4, 2, 2, 2, 2, 2), AXES)
    in_specs = (
        P(AXES, None),
        P(),
        P(FS, None, TP),
        P(FS, TP),
        P(),
        P(FS, None, TP),
        P(FS, TP),
        P(AXES, None),
    )
    out_specs = (
        P(AXES, None),
        P(AXES, None),
        P(),
        P(FS, None, TP),
        P(FS, TP),
        P(),
        P(FS, None, TP),
        P(FS, TP),
    )
    return jax.shard_map(
        on_device, mesh=fine, in_specs=in_specs, out_specs=out_specs, check_vma=False
    )
```

```python
import functools

import jax
import jax.numpy as jnp
import numpy as np
from jax import lax
from jax.experimental import pallas as pl
from jax.experimental.pallas import tpu as pltpu
from jax.sharding import Mesh
from jax.sharding import PartitionSpec as P

HD = 64
LEN = 1280
EPSILON = 1e-05
THETA = 160000.0
ROWS = 160
WIDTH = 1024
FFB = 328
PAD = 384
QB = 256
VMEM = 60 * 1024 * 1024

AXES = ("x", "zl", "c", "yh", "yl", "zh")
FS = ("x", "zl", "c")
TP = ("yh", "yl", "zh")
MLP_AX = ("yh", "yl")
PRE_AX = ("zh",)
M = 4
PRE = 2
F32 = jnp.float32
BF16 = jnp.bfloat16


def exchange(value, axes, count, mask):
    return lax.ppermute(value, axes, [(i, i ^ mask) for i in range(count)])


def gather_by_mask(value, axes, count):
    return [value] + [exchange(value, axes, count, m) for m in range(1, count)]


def scatter_by_mask(parts, axes, count):
    return [parts[0]] + [exchange(parts[m], axes, count, m) for m in range(1, count)]


def total(parts):
    result = parts[0].astype(F32)
    for part in parts[1:]:
        result = result + part.astype(F32)
    return result


def normalize(values):
    centre = values - jnp.mean(values, axis=-1, keepdims=True)
    scaling = lax.rsqrt(jnp.mean(centre * centre, axis=-1, keepdims=True) + EPSILON)
    return (centre * scaling, scaling)


def norm_back(grad_normed, normed_hat, scaling, gain):
    grad_hat = grad_normed * gain
    mean_grad = jnp.mean(grad_hat, axis=-1, keepdims=True)
    mean_proj = jnp.mean(grad_hat * normed_hat, axis=-1, keepdims=True)
    return (
        scaling * (grad_hat - mean_grad - normed_hat * mean_proj),
        jnp.sum(grad_normed * normed_hat, axis=0),
    )


def rope_tables():
    half = HD // 2
    freqs = THETA ** (-np.arange(half) * 2.0 / HD)
    angles = np.arange(LEN)[:, None] * freqs[None, :]
    cosine, sine = np.cos(angles), np.sin(angles)
    return (
        jnp.asarray(np.concatenate([cosine] * 4, axis=1), F32),
        jnp.asarray(np.concatenate([-sine, sine, -sine, sine], axis=1), F32),
    )


def dot(a, b, ca, cb):
    return lax.dot_general(a, b, (((ca,), (cb,)), ((), ())), preferred_element_type=F32)


def swap_halves(values):
    lane = lax.broadcasted_iota(jnp.int32, values.shape, 1)
    first = (lane // 32) % 2 == 0
    return jnp.where(first, pltpu.roll(values, 96, 1), pltpu.roll(values, 32, 1))


def head_mask(values, head):
    lane = lax.broadcasted_iota(jnp.int32, values.shape, 1)
    return jnp.where((lane // HD) == head, values, jnp.zeros_like(values))


def attend_kernel(
    rows_ref, w_ref, cos_ref, sin_ref, q_ref, k_ref, v_ref, mixed_ref, lse_ref, proj
):
    proj[...] = dot(rows_ref[...].reshape(LEN, WIDTH), w_ref[...].reshape(WIDTH, PAD), 1, 0)
    cosine, sine = cos_ref[...], sin_ref[...]
    value = proj[:, : 2 * HD]
    value = value * cosine + swap_halves(value) * sine
    q_ref[...] = value.astype(BF16) * jnp.asarray(0.125, BF16)
    value = proj[:, 2 * HD : 4 * HD]
    k_ref[...] = (value * cosine + swap_halves(value) * sine).astype(BF16)
    v_ref[...] = proj[:, 4 * HD :].astype(BF16)

    def block(i, carry):
        at = pl.ds(pl.multiple_of(i * QB, QB), QB)
        query = q_ref[at, :]
        outs = []
        sums = []
        for head in range(2):
            scores = dot(head_mask(query, head), k_ref[...], 1, 1)
            peak = jnp.max(scores, axis=1, keepdims=True)
            exponent = jnp.exp(scores - peak)
            row_sum = jnp.sum(exponent, axis=1, keepdims=True)
            out = dot(exponent.astype(BF16), v_ref[...], 1, 0)
            outs.append(out / row_sum)
            sums.append(jnp.broadcast_to(peak + jnp.log(row_sum), (QB, 2 * HD)))
        lane = lax.broadcasted_iota(jnp.int32, (QB, 2 * HD), 1)
        mixed_ref[at, :] = jnp.where(lane < HD, outs[0], outs[1]).astype(BF16)
        lse_ref[at, :] = jnp.where(lane < HD, sums[0], sums[1])
        return carry

    lax.fori_loop(0, LEN // QB, block, 0)


def whole(*shape):
    return pl.BlockSpec(shape, lambda i: (0,) * len(shape))


ROWS_SPEC = pl.BlockSpec((8, ROWS, WIDTH), lambda i: (0, 0, 0))
QKV_SPEC = pl.BlockSpec((16, 1, 64, PAD), lambda i: (0, 3, 0, 0))


def attend(rows, weights, cosine, sine):
    wide = jax.ShapeDtypeStruct((LEN, 2 * HD), BF16)
    return pl.pallas_call(
        attend_kernel,
        grid=(1,),
        in_specs=[ROWS_SPEC, QKV_SPEC, whole(LEN, 2 * HD), whole(LEN, 2 * HD)],
        out_specs=[whole(LEN, 2 * HD)] * 5,
        out_shape=[wide, wide, wide, wide, jax.ShapeDtypeStruct((LEN, 2 * HD), F32)],
        scratch_shapes=[pltpu.VMEM((LEN, PAD), F32)],
        compiler_params=pltpu.CompilerParams(vmem_limit_bytes=VMEM),
        cost_estimate=pl.CostEstimate(
            flops=6_000_000_000, bytes_accessed=8_000_000, transcendentals=3_300_000
        ),
        name="attend",
    )(rows, weights, cosine, sine)


def attend_back_kernel(me_ref, *refs):
    q_ref, k_ref, v_ref, lse_ref, g_ref, cos_ref, sin_ref, w_ref, out_ref = refs[:9]
    dn_refs = refs[9:17]
    key_sum, val_sum, dn = refs[17:]
    key_sum[...] = jnp.zeros_like(key_sum)
    val_sum[...] = jnp.zeros_like(val_sum)

    def block(i, carry):
        at = pl.ds(pl.multiple_of(i * QB, QB), QB)
        query = q_ref[at, :]
        grad = g_ref[at, :]
        grad_query = jnp.zeros((QB, 2 * HD), F32)
        for head in range(2):
            query_h = head_mask(query, head)
            grad_h = head_mask(grad, head)
            scores = dot(query_h, k_ref[...], 1, 1)
            probs = jnp.exp(scores - lse_ref[at, head * HD : head * HD + 1])
            grad_probs = dot(grad_h, v_ref[...], 1, 1)
            inner = jnp.sum(grad_probs * probs, axis=1, keepdims=True)
            grad_scores = (probs * (grad_probs - inner)).astype(BF16)
            grad_query = grad_query + dot(grad_scores, head_mask(k_ref[...], head), 1, 0)
            key_sum[...] += dot(query_h, grad_scores, 0, 0)
            val_sum[...] += dot(grad_h, probs.astype(BF16), 0, 0)
        grad_query = grad_query * 0.125
        cosine, sine = cos_ref[at, :], sin_ref[at, :]
        grad_query = grad_query * cosine - swap_halves(grad_query) * sine
        out_ref[at, : 2 * HD] = grad_query.astype(BF16)
        return carry

    lax.fori_loop(0, LEN // QB, block, 0)
    grad_key = key_sum[...].T
    grad_key = grad_key * cos_ref[...] - swap_halves(grad_key) * sin_ref[...]
    out_ref[:, 2 * HD : 4 * HD] = grad_key.astype(BF16)
    out_ref[:, 4 * HD :] = val_sum[...].T.astype(BF16)
    dn[...] = dot(out_ref[...], w_ref[...].reshape(WIDTH, PAD), 1, 1).astype(BF16)
    me = me_ref[0]
    for m in range(8):
        at = pl.multiple_of(jnp.bitwise_xor(me, m) * ROWS, ROWS)
        dn_refs[m][...] = dn[pl.ds(at, ROWS), :]


def attend_back(me, q, k, v, lse, grad_mixed, cosine, sine, weights):
    return pl.pallas_call(
        attend_back_kernel,
        grid=(1,),
        in_specs=[pl.BlockSpec(memory_space=pltpu.SMEM)]
        + [whole(LEN, 2 * HD)] * 7
        + [QKV_SPEC],
        out_specs=[whole(LEN, PAD)] + [whole(ROWS, WIDTH)] * 8,
        out_shape=[jax.ShapeDtypeStruct((LEN, PAD), BF16)]
        + [jax.ShapeDtypeStruct((ROWS, WIDTH), BF16)] * 8,
        scratch_shapes=[
            pltpu.VMEM((2 * HD, LEN), F32),
            pltpu.VMEM((2 * HD, LEN), F32),
            pltpu.VMEM((LEN, WIDTH), BF16),
        ],
        compiler_params=pltpu.CompilerParams(vmem_limit_bytes=VMEM),
        cost_estimate=pl.CostEstimate(
            flops=12_000_000_000, bytes_accessed=8_000_000, transcendentals=3_300_000
        ),
        name="attend_back",
    )(me, q, k, v, lse, grad_mixed, cosine, sine, weights)


def qkv_grads_kernel(rows_ref, g_ref, out_ref, turned):
    for r in range(8):
        turned[:, r * ROWS : (r + 1) * ROWS] = rows_ref[r].T
    out_ref[...] = dot(turned[...], g_ref[...], 1, 0).astype(BF16).reshape(16, 64, PAD)


def qkv_grads(rows, grad_qkv):
    return pl.pallas_call(
        qkv_grads_kernel,
        grid=(1,),
        in_specs=[ROWS_SPEC, whole(LEN, PAD)],
        out_specs=whole(16, 64, PAD),
        out_shape=jax.ShapeDtypeStruct((16, 64, PAD), BF16),
        scratch_shapes=[pltpu.VMEM((WIDTH, LEN), BF16)],
        compiler_params=pltpu.CompilerParams(vmem_limit_bytes=VMEM),
        cost_estimate=pl.CostEstimate(
            flops=2_000_000_000, bytes_accessed=5_000_000, transcendentals=0
        ),
        name="qkv_grads",
    )(rows, grad_qkv)


def store_by_owner(ref, at, value):
    value = value.astype(BF16)
    for x in range(4):
        for zl in range(2):
            for c in range(2):
                row = (x * 4 + zl * 2 + c) * 64
                ref[x * 2 + c, zl, at] = value[row : row + 64, :]


def mlp_kernel(count, *refs):
    row_refs, back_refs = refs[:count], refs[count : 2 * count]
    w0_ref, w1_ref, act_ref, gh_ref = refs[2 * count : 2 * count + 4]
    dn_refs = refs[2 * count + 4 : 3 * count + 4]
    rows, back, dn = refs[3 * count + 4 :]
    for r in range(count):
        rows[r * ROWS : (r + 1) * ROWS, :] = row_refs[r][...]
        back[r * ROWS : (r + 1) * ROWS, :] = back_refs[r][...]
    for step, w_ref in enumerate((w0_ref, w1_ref)):
        w_act = w_ref[:, 0].reshape(WIDTH, PAD)
        w_gate = w_ref[:, 1].reshape(WIDTH, PAD)
        w_down = w_ref[:, 2].reshape(WIDTH, PAD)
        a_in = dot(rows[...], w_act, 1, 0)
        gate = dot(rows[...], w_gate, 1, 0)
        grad_act = dot(back[...], w_down, 1, 0)
        cdf = 0.5 * (1.0 + lax.erf(a_in * (0.5**0.5)))
        gelu = a_in * cdf
        slope = cdf + a_in * (jnp.exp(-0.5 * a_in * a_in) * 0.3989422804014327)
        act_ref[step] = (gelu * gate).astype(BF16)
        g_act = (grad_act * gate * slope).astype(BF16)
        g_gate = (grad_act * gelu).astype(BF16)
        gh_ref[step, 0] = g_act
        gh_ref[step, 1] = g_gate
        part = dot(g_act, w_act, 1, 1) + dot(g_gate, w_gate, 1, 1)
        if step == 0:
            dn[...] = part
        else:
            dn[...] += part
    for r in range(count):
        dn_refs[r][...] = dn[r * ROWS : (r + 1) * ROWS, :].astype(BF16)


MLP_SPEC = pl.BlockSpec((16, 3, 64, PAD), lambda p: (0, 0, 0, 0))
MORE_SPEC = pl.BlockSpec((16, 3, 64, PAD), lambda p: (0, 1, 0, 0))
DOWN_SPEC = pl.BlockSpec((16, 1, 64, PAD), lambda p: (0, 2, 0, 0))
DOWN_MORE_SPEC = pl.BlockSpec((16, 1, 64, PAD), lambda p: (0, 5, 0, 0))


def act_spec(count):
    return pl.BlockSpec((1, count * ROWS, PAD), lambda p: (p, 0, 0))


def hidden_spec(count):
    return pl.BlockSpec((1, 2, count * ROWS, PAD), lambda p: (p, 0, 0, 0))


def mlp(row_blocks, back_blocks, weights):
    count = len(row_blocks)
    group = count * ROWS
    return pl.pallas_call(
        functools.partial(mlp_kernel, count),
        grid=(1,),
        in_specs=[whole(ROWS, WIDTH)] * (2 * count) + [MLP_SPEC, MORE_SPEC],
        out_specs=[whole(PRE, group, PAD), whole(PRE, 2, group, PAD)]
        + [whole(ROWS, WIDTH)] * count,
        out_shape=[
            jax.ShapeDtypeStruct((PRE, group, PAD), BF16),
            jax.ShapeDtypeStruct((PRE, 2, group, PAD), BF16),
        ]
        + [jax.ShapeDtypeStruct((ROWS, WIDTH), BF16)] * count,
        scratch_shapes=[
            pltpu.VMEM((group, WIDTH), BF16),
            pltpu.VMEM((group, WIDTH), BF16),
            pltpu.VMEM((group, WIDTH), F32),
        ],
        compiler_params=pltpu.CompilerParams(vmem_limit_bytes=VMEM),
        cost_estimate=pl.CostEstimate(
            flops=5_000_000_000, bytes_accessed=8_000_000, transcendentals=500_000
        ),
        name="mlp",
    )(*row_blocks, *back_blocks, weights, weights)


def mlp_grads_kernel(*refs):
    row_refs, back_refs = refs[:M], refs[M : 2 * M]
    w0_ref, w1_ref, act0_ref, act1_ref, gh0_ref, gh1_ref, grad_ref = refs[2 * M : 2 * M + 7]
    sum_refs = refs[2 * M + 7 : 3 * M + 7]
    rows, back, sums = refs[3 * M + 7 :]
    step = pl.program_id(0)
    half = M // 2 * ROWS

    @pl.when(step == 0)
    def _():
        for r in range(M):
            rows[:, r * ROWS : (r + 1) * ROWS] = row_refs[r][...].T
            back[:, r * ROWS : (r + 1) * ROWS] = back_refs[r][...].T
        w_down = w0_ref[...].reshape(WIDTH, PAD)
        sums[:half] = dot(act0_ref[0], w_down, 1, 1)
        sums[half:] = dot(act1_ref[0], w_down, 1, 1)

    act = jnp.concatenate([act0_ref[0], act1_ref[0]], axis=0)
    for c in range(2):
        grad_hidden = jnp.concatenate([gh0_ref[0, c], gh1_ref[0, c]], axis=0)
        store_by_owner(grad_ref, c, dot(rows[...], grad_hidden, 1, 0))
    store_by_owner(grad_ref, 2, dot(back[...], act, 1, 0))

    @pl.when(step == 1)
    def _():
        w_down = w1_ref[...].reshape(WIDTH, PAD)
        sums[:half] += dot(act0_ref[0], w_down, 1, 1)
        sums[half:] += dot(act1_ref[0], w_down, 1, 1)
        for r in range(M):
            sum_refs[r][...] = sums[r * ROWS : (r + 1) * ROWS, :].astype(BF16)


def mlp_grads(row_blocks, back_blocks, weights, acts, grads_hidden):
    group = M * ROWS
    return pl.pallas_call(
        mlp_grads_kernel,
        grid=(PRE,),
        in_specs=[whole(ROWS, WIDTH)] * (2 * M)
        + [DOWN_SPEC, DOWN_MORE_SPEC]
        + [act_spec(M // 2)] * 2
        + [hidden_spec(M // 2)] * 2,
        out_specs=[pl.BlockSpec((8, 2, 3, 64, PAD), lambda p: (0, 0, p, 0, 0))]
        + [whole(ROWS, WIDTH)] * M,
        out_shape=[jax.ShapeDtypeStruct((8, 2, 3 * PRE + 3, 64, PAD), BF16)]
        + [jax.ShapeDtypeStruct((ROWS, WIDTH), BF16)] * M,
        scratch_shapes=[
            pltpu.VMEM((WIDTH, group), BF16),
            pltpu.VMEM((WIDTH, group), BF16),
            pltpu.VMEM((group, WIDTH), F32),
        ],
        compiler_params=pltpu.CompilerParams(vmem_limit_bytes=VMEM),
        cost_estimate=pl.CostEstimate(
            flops=8_000_000_000, bytes_accessed=12_000_000, transcendentals=0
        ),
        name="mlp_grads",
    )(*row_blocks, *back_blocks, weights, weights, *acts, *grads_hidden)


def out_grads_kernel(g_ref, mixed_ref, held_ref, grad_ref):
    del held_ref
    turned = g_ref[...].T
    for b in range(3):
        columns = mixed_ref[:, b * PAD : (b + 1) * PAD]
        store_by_owner(grad_ref, b, dot(turned, columns, 1, 0))


def out_grads(grad_attn, mixed_own, grads):
    return pl.pallas_call(
        out_grads_kernel,
        grid=(1,),
        in_specs=[whole(ROWS, WIDTH), whole(ROWS, 3 * PAD), pl.BlockSpec(memory_space=pl.ANY)],
        out_specs=pl.BlockSpec((8, 2, 3, 64, PAD), lambda p: (0, 0, PRE, 0, 0)),
        out_shape=jax.ShapeDtypeStruct(grads.shape, BF16),
        input_output_aliases={2: 0},
        compiler_params=pltpu.CompilerParams(vmem_limit_bytes=VMEM),
        cost_estimate=pl.CostEstimate(
            flops=400_000_000, bytes_accessed=4_000_000, transcendentals=0
        ),
        name="out_grads",
    )(grad_attn, mixed_own, grads)


def two_parts(value):
    high = value.astype(BF16)
    return high, (value - high.astype(F32)).astype(BF16)


def on_device(tokens, gain_attn, w_qkv, w_out, gain_mlp, w_in, w_down, cotangent):
    own_mlp = jnp.concatenate([w_in, w_down[:, None, :]], axis=1).transpose(1, 0, 2)
    own_mlp = jnp.pad(own_mlp, ((0, 0), (0, 0), (0, PAD - FFB)))
    own_qkv = w_qkv.reshape(64, PAD)
    out_wide = lax.all_to_all(jnp.broadcast_to(w_out[None], (8, 64, 2 * HD)), TP, 0, 0)
    out_wide = out_wide.transpose(1, 0, 2).reshape(64, WIDTH)
    out_wide = jnp.concatenate([out_wide, jnp.zeros((64, 2 * HD), BF16), own_qkv], axis=1)
    out_wide = out_wide.reshape(64, 4, PAD).transpose(1, 0, 2)
    weights = lax.all_gather(out_wide, FS, axis=0)
    partner_mlp = exchange(own_mlp, PRE_AX, PRE, 1)
    weights_mlp = lax.all_gather(jnp.concatenate([own_mlp, partner_mlp], axis=0), FS, axis=0)
    cosine, sine = rope_tables()

    resid = tokens.astype(F32)
    hat_attn, scale_attn = normalize(resid)
    normed_attn = (hat_attn * gain_attn).astype(BF16)
    partner_rows = exchange(normed_attn, PRE_AX, PRE, 1)
    first = lax.axis_index("zh") == 0
    pair = jnp.stack(
        [
            jnp.where(first, normed_attn, partner_rows),
            jnp.where(first, partner_rows, normed_attn),
        ]
    )
    rows = lax.all_to_all(jnp.broadcast_to(pair[None], (M, PRE, ROWS, WIDTH)), MLP_AX, 0, 0)
    rows = rows.reshape(8, ROWS, WIDTH)

    cotangent_later, rows = lax.optimization_barrier((cotangent, rows))
    back_blocks = gather_by_mask(cotangent_later, MLP_AX, M)
    q, k, v, mixed, lse = attend(rows, weights, cosine, sine)
    mixed, *back_blocks = lax.optimization_barrier((mixed, *back_blocks))
    mixed_own = lax.all_to_all(mixed.reshape(8, ROWS, 2 * HD), TP, 0, 0)
    mixed_own = mixed_own.transpose(1, 0, 2).reshape(ROWS, WIDTH)
    mixed_own = jnp.pad(mixed_own, ((0, 0), (0, 3 * PAD - WIDTH)))
    full_out = [weights[:, b].reshape(WIDTH, PAD) for b in range(3)]
    attn_sum = sum(
        dot(mixed_own[:, b * PAD : (b + 1) * PAD], full_out[b], 1, 1) for b in range(3)
    )
    resid_mid = resid + attn_sum
    hat_mlp, scale_mlp = normalize(resid_mid)
    normed_mlp = (hat_mlp * gain_mlp).astype(BF16)

    row_blocks = gather_by_mask(normed_mlp, MLP_AX, M)
    act0, hidden0, *dn0 = mlp(row_blocks[:2], back_blocks[:2], weights_mlp)
    *later, dn0[1] = lax.optimization_barrier((*row_blocks[2:], dn0[1]))
    row_blocks = row_blocks[:2] + later
    act1, hidden1, *dn1 = mlp(row_blocks[2:], back_blocks[2:], weights_mlp)
    grad_normed_mlp = total(scatter_by_mask(dn0 + dn1, MLP_AX, M))
    grads, *sum_parts = mlp_grads(
        row_blocks, back_blocks, weights_mlp, (act0, act1), (hidden0, hidden1)
    )

    grad_mid_norm, gain_mlp_part = norm_back(grad_normed_mlp, hat_mlp, scale_mlp, gain_mlp)
    grad_mid = cotangent.astype(F32) + grad_mid_norm
    grad_attn = grad_mid.astype(BF16)
    grad_mixed = jnp.concatenate([dot(grad_attn, full_out[b], 1, 0) for b in range(3)], axis=1)
    grad_mixed = grad_mixed[:, :WIDTH].astype(BF16)
    gm_parts = grad_mixed.reshape(ROWS, 8, 2 * HD).transpose(1, 0, 2)
    grads = out_grads(grad_attn, mixed_own, grads)
    grads = lax.psum_scatter(grads, ("x", "c"), scatter_dimension=0)
    gm_own = lax.all_to_all(gm_parts, TP, 0, 0).reshape(LEN, 2 * HD)

    *sum_parts, gm_own = lax.optimization_barrier((*sum_parts, gm_own))
    sum_parts = scatter_by_mask(sum_parts, MLP_AX, M)
    me = lax.axis_index(TP).astype(jnp.int32)[None]
    grad_qkv, *dn_attn_parts = attend_back(
        me, q, k, v, lse, gm_own, cosine, sine, weights
    )
    held = lax.optimization_barrier((*sum_parts, *dn_attn_parts))
    sum_parts, dn_attn_parts = held[:M], held[M:]
    layer_out = (resid_mid + total(sum_parts)).astype(BF16)
    received = scatter_by_mask(dn_attn_parts, TP, 8)

    qkv_part = qkv_grads(rows, grad_qkv)
    high, low = two_parts(gain_mlp_part.reshape(16, 1, 64))
    extra = jnp.pad(jnp.concatenate([high, low], axis=1), ((0, 0), (0, 14), (0, PAD - 64)))
    got = lax.all_to_all(jnp.concatenate([qkv_part, extra], axis=1), FS, 0, 0)
    got = jnp.sum(got.astype(F32), axis=0)
    grad_qkv_w = got[:64]
    gain_mlp_own = got[64, :64] + got[65, :64]
    gain_own = lax.dynamic_slice_in_dim(gain_attn, lax.axis_index(FS) * 64, 64)
    gain_attn_own = jnp.sum(grad_qkv_w * own_qkv.astype(F32), axis=1) / gain_own
    gains = jnp.concatenate([gain_attn_own, gain_mlp_own])
    bit = lax.axis_index("zl")
    keep = lax.dynamic_index_in_dim(grads, bit, 0, keepdims=False)
    send = lax.dynamic_index_in_dim(grads, 1 - bit, 0, keepdims=False)
    halves = keep.astype(F32) + exchange(send, ("zl",), 2, 1).astype(F32)
    from_partner = exchange(halves[3:6].astype(BF16), PRE_AX, PRE, 1)
    grad_mlp = halves[:3] + from_partner.astype(F32)
    grad_in = grad_mlp[:2, :, :FFB].transpose(1, 0, 2)
    grad_down = grad_mlp[2, :, :FFB]
    out_parts = halves[6:].astype(BF16).transpose(1, 0, 2).reshape(64, 3 * PAD)[:, :WIDTH]
    out_parts = out_parts.reshape(64, 8, 2 * HD).transpose(1, 0, 2)
    gains = jnp.broadcast_to(gains[None, None], (128, 1, 128))
    gains = lax.all_to_all(gains, AXES, 0, 0).reshape(16, 8, 128).sum(axis=1)
    grad_out = jnp.sum(lax.all_to_all(out_parts, TP, 0, 0).astype(F32), axis=0)

    grad_normed_attn = total(received)
    grad_first, _ = norm_back(grad_normed_attn, hat_attn, scale_attn, gain_attn)
    grad_tokens = (grad_mid + grad_first).astype(BF16)
    return (
        layer_out,
        grad_tokens,
        gains[:, :64].reshape(WIDTH),
        grad_qkv_w.reshape(64, 3, 2 * HD),
        grad_out,
        gains[:, 64:].reshape(WIDTH),
        grad_in,
        grad_down,
    )


def solution(mesh):
    fine = Mesh(mesh.devices.reshape(4, 2, 2, 2, 2, 2), AXES)
    in_specs = (
        P(AXES, None),
        P(),
        P(FS, None, TP),
        P(FS, TP),
        P(),
        P(FS, None, TP),
        P(FS, TP),
        P(AXES, None),
    )
    out_specs = (
        P(AXES, None),
        P(AXES, None),
        P(),
        P(FS, None, TP),
        P(FS, TP),
        P(),
        P(FS, None, TP),
        P(FS, TP),
    )
    return jax.shard_map(
        on_device, mesh=fine, in_specs=in_specs, out_specs=out_specs, check_vma=False
    )
```

```python
import functools

import jax
import jax.numpy as jnp
import numpy as np
from jax import lax
from jax.experimental import pallas as pl
from jax.experimental.pallas import tpu as pltpu
from jax.sharding import Mesh
from jax.sharding import PartitionSpec as P

HD = 64
LEN = 1280
EPSILON = 1e-05
THETA = 160000.0
ROWS = 160
WIDTH = 1024
FFB = 328
PAD = 384
QB = 256
BACK_QB = 320
VMEM = 60 * 1024 * 1024

AXES = ("x", "zl", "c", "yh", "yl", "zh")
FS = ("x", "zl", "c")
TP = ("yh", "yl", "zh")
MLP_AX = ("yh", "yl")
PRE_AX = ("zh",)
M = 4
PRE = 2
F32 = jnp.float32
BF16 = jnp.bfloat16


def exchange(value, axes, count, mask):
    return lax.ppermute(value, axes, [(i, i ^ mask) for i in range(count)])


def gather_by_mask(value, axes, count):
    return [value] + [exchange(value, axes, count, m) for m in range(1, count)]


def scatter_by_mask(parts, axes, count):
    return [parts[0]] + [exchange(parts[m], axes, count, m) for m in range(1, count)]


def total(parts):
    result = parts[0].astype(F32)
    for part in parts[1:]:
        result = result + part.astype(F32)
    return result


def normalize(values):
    centre = values - jnp.mean(values, axis=-1, keepdims=True)
    scaling = lax.rsqrt(jnp.mean(centre * centre, axis=-1, keepdims=True) + EPSILON)
    return (centre * scaling, scaling)


def norm_back(grad_normed, normed_hat, scaling, gain):
    grad_hat = grad_normed * gain
    mean_grad = jnp.mean(grad_hat, axis=-1, keepdims=True)
    mean_proj = jnp.mean(grad_hat * normed_hat, axis=-1, keepdims=True)
    return (
        scaling * (grad_hat - mean_grad - normed_hat * mean_proj),
        jnp.sum(grad_normed * normed_hat, axis=0),
    )


def rope_tables():
    half = HD // 2
    freqs = THETA ** (-np.arange(half) * 2.0 / HD)
    angles = np.arange(LEN)[:, None] * freqs[None, :]
    cosine, sine = np.cos(angles), np.sin(angles)
    return (
        jnp.asarray(np.concatenate([cosine] * 4, axis=1), F32),
        jnp.asarray(np.concatenate([-sine, sine, -sine, sine], axis=1), F32),
    )


def by_head(values):
    lane = lax.broadcasted_iota(jnp.int32, values.shape, 1)
    zeros = jnp.zeros_like(values)
    return jnp.concatenate(
        [jnp.where(lane < HD, values, zeros), jnp.where(lane < HD, zeros, values)], axis=0
    )


def dot(a, b, ca, cb):
    return lax.dot_general(a, b, (((ca,), (cb,)), ((), ())), preferred_element_type=F32)


def swap_halves(values):
    lane = lax.broadcasted_iota(jnp.int32, values.shape, 1)
    first = (lane // 32) % 2 == 0
    return jnp.where(first, pltpu.roll(values, 96, 1), pltpu.roll(values, 32, 1))


def head_mask(values, head):
    lane = lax.broadcasted_iota(jnp.int32, values.shape, 1)
    return jnp.where((lane // HD) == head, values, jnp.zeros_like(values))


def attend_kernel(
    rows_ref, w_ref, cos_ref, sin_ref, q_ref, k_ref, v_ref, mixed_ref, lse_ref, proj
):
    proj[...] = dot(rows_ref[...].reshape(LEN, WIDTH), w_ref[...].reshape(WIDTH, PAD), 1, 0)
    cosine, sine = cos_ref[...], sin_ref[...]
    value = proj[:, : 2 * HD]
    value = value * cosine + swap_halves(value) * sine
    q_ref[...] = value.astype(BF16) * jnp.asarray(0.125, BF16)
    value = proj[:, 2 * HD : 4 * HD]
    k_ref[...] = (value * cosine + swap_halves(value) * sine).astype(BF16)
    v_ref[...] = proj[:, 4 * HD :].astype(BF16)

    def block(i, carry):
        at = pl.ds(pl.multiple_of(i * QB, QB), QB)
        query = q_ref[at, :]
        outs = []
        sums = []
        for head in range(2):
            scores = dot(head_mask(query, head), k_ref[...], 1, 1)
            peak = jnp.max(scores, axis=1, keepdims=True)
            exponent = jnp.exp(scores - peak)
            row_sum = jnp.sum(exponent, axis=1, keepdims=True)
            out = dot(exponent.astype(BF16), v_ref[...], 1, 0)
            outs.append(out / row_sum)
            sums.append(jnp.broadcast_to(peak + jnp.log(row_sum), (QB, 2 * HD)))
        lane = lax.broadcasted_iota(jnp.int32, (QB, 2 * HD), 1)
        mixed_ref[at, :] = jnp.where(lane < HD, outs[0], outs[1]).astype(BF16)
        lse_ref[at, :] = jnp.where(lane < HD, sums[0], sums[1])
        return carry

    lax.fori_loop(0, LEN // QB, block, 0)


def whole(*shape):
    return pl.BlockSpec(shape, lambda i: (0,) * len(shape))


ROWS_SPEC = pl.BlockSpec((8, ROWS, WIDTH), lambda i: (0, 0, 0))
QKV_SPEC = pl.BlockSpec((16, 1, 64, PAD), lambda i: (0, 3, 0, 0))


def attend(rows, weights, cosine, sine):
    wide = jax.ShapeDtypeStruct((LEN, 2 * HD), BF16)
    return pl.pallas_call(
        attend_kernel,
        grid=(1,),
        in_specs=[ROWS_SPEC, QKV_SPEC, whole(LEN, 2 * HD), whole(LEN, 2 * HD)],
        out_specs=[whole(LEN, 2 * HD)] * 5,
        out_shape=[wide, wide, wide, wide, jax.ShapeDtypeStruct((LEN, 2 * HD), F32)],
        scratch_shapes=[pltpu.VMEM((LEN, PAD), F32)],
        compiler_params=pltpu.CompilerParams(vmem_limit_bytes=VMEM),
        cost_estimate=pl.CostEstimate(
            flops=6_000_000_000, bytes_accessed=8_000_000, transcendentals=3_300_000
        ),
        name="attend",
    )(rows, weights, cosine, sine)


def attend_back_kernel(me_ref, *refs):
    q_ref, k_ref, v_ref, lse_ref, g_ref, cos_ref, sin_ref, w_ref, out_ref = refs[:9]
    dn_refs = refs[9:17]
    key_sum, val_sum, dn = refs[17:]
    key_sum[...] = jnp.zeros_like(key_sum)
    val_sum[...] = jnp.zeros_like(val_sum)

    def block(i, carry):
        at = pl.ds(pl.multiple_of(i * BACK_QB, BACK_QB), BACK_QB)
        query = by_head(q_ref[at, :])
        grad = by_head(g_ref[at, :])
        logs = jnp.concatenate([lse_ref[at, :1], lse_ref[at, HD : HD + 1]], axis=0)
        probs = jnp.exp(dot(query, k_ref[...], 1, 1) - logs)
        grad_probs = dot(grad, v_ref[...], 1, 1)
        inner = jnp.sum(grad_probs * probs, axis=1, keepdims=True)
        grad_scores = (probs * (grad_probs - inner)).astype(BF16)
        both = dot(grad_scores, k_ref[...], 1, 0)
        lane = lax.broadcasted_iota(jnp.int32, (BACK_QB, 2 * HD), 1)
        grad_query = jnp.where(lane < HD, both[:BACK_QB], both[BACK_QB:])
        key_sum[...] += dot(query, grad_scores, 0, 0)
        val_sum[...] += dot(grad, probs.astype(BF16), 0, 0)
        grad_query = grad_query * 0.125
        cosine, sine = cos_ref[at, :], sin_ref[at, :]
        grad_query = grad_query * cosine - swap_halves(grad_query) * sine
        out_ref[at, : 2 * HD] = grad_query.astype(BF16)
        return carry

    lax.fori_loop(0, LEN // BACK_QB, block, 0)
    grad_key = key_sum[...].T
    grad_key = grad_key * cos_ref[...] - swap_halves(grad_key) * sin_ref[...]
    out_ref[:, 2 * HD : 4 * HD] = grad_key.astype(BF16)
    out_ref[:, 4 * HD :] = val_sum[...].T.astype(BF16)
    dn[...] = dot(out_ref[...], w_ref[...].reshape(WIDTH, PAD), 1, 1).astype(BF16)
    me = me_ref[0]
    for m in range(8):
        at = pl.multiple_of(jnp.bitwise_xor(me, m) * ROWS, ROWS)
        dn_refs[m][...] = dn[pl.ds(at, ROWS), :]


def attend_back(me, q, k, v, lse, grad_mixed, cosine, sine, weights):
    return pl.pallas_call(
        attend_back_kernel,
        grid=(1,),
        in_specs=[pl.BlockSpec(memory_space=pltpu.SMEM)]
        + [whole(LEN, 2 * HD)] * 7
        + [QKV_SPEC],
        out_specs=[whole(LEN, PAD)] + [whole(ROWS, WIDTH)] * 8,
        out_shape=[jax.ShapeDtypeStruct((LEN, PAD), BF16)]
        + [jax.ShapeDtypeStruct((ROWS, WIDTH), BF16)] * 8,
        scratch_shapes=[
            pltpu.VMEM((2 * HD, LEN), F32),
            pltpu.VMEM((2 * HD, LEN), F32),
            pltpu.VMEM((LEN, WIDTH), BF16),
        ],
        compiler_params=pltpu.CompilerParams(vmem_limit_bytes=VMEM),
        cost_estimate=pl.CostEstimate(
            flops=12_000_000_000, bytes_accessed=8_000_000, transcendentals=3_300_000
        ),
        name="attend_back",
    )(me, q, k, v, lse, grad_mixed, cosine, sine, weights)


def qkv_grads_kernel(rows_ref, g_ref, out_ref, turned):
    for r in range(8):
        turned[:, r * ROWS : (r + 1) * ROWS] = rows_ref[r].T
    out_ref[...] = dot(turned[...], g_ref[...], 1, 0).astype(BF16).reshape(16, 64, PAD)


def qkv_grads(rows, grad_qkv):
    return pl.pallas_call(
        qkv_grads_kernel,
        grid=(1,),
        in_specs=[ROWS_SPEC, whole(LEN, PAD)],
        out_specs=whole(16, 64, PAD),
        out_shape=jax.ShapeDtypeStruct((16, 64, PAD), BF16),
        scratch_shapes=[pltpu.VMEM((WIDTH, LEN), BF16)],
        compiler_params=pltpu.CompilerParams(vmem_limit_bytes=VMEM),
        cost_estimate=pl.CostEstimate(
            flops=2_000_000_000, bytes_accessed=5_000_000, transcendentals=0
        ),
        name="qkv_grads",
    )(rows, grad_qkv)


def store_by_owner(ref, at, value):
    value = value.astype(BF16)
    for x in range(4):
        for zl in range(2):
            for c in range(2):
                row = (x * 4 + zl * 2 + c) * 64
                ref[x * 2 + c, zl, at] = value[row : row + 64, :]


def mlp_kernel(count, *refs):
    row_refs, back_refs = refs[:count], refs[count : 2 * count]
    w0_ref, w1_ref, act_ref, gh_ref = refs[2 * count : 2 * count + 4]
    dn_refs = refs[2 * count + 4 : 3 * count + 4]
    rows, back, dn = refs[3 * count + 4 :]
    for r in range(count):
        rows[r * ROWS : (r + 1) * ROWS, :] = row_refs[r][...]
        back[r * ROWS : (r + 1) * ROWS, :] = back_refs[r][...]
    for step, w_ref in enumerate((w0_ref, w1_ref)):
        w_act = w_ref[:, 0].reshape(WIDTH, PAD)
        w_gate = w_ref[:, 1].reshape(WIDTH, PAD)
        w_down = w_ref[:, 2].reshape(WIDTH, PAD)
        a_in = dot(rows[...], w_act, 1, 0)
        gate = dot(rows[...], w_gate, 1, 0)
        grad_act = dot(back[...], w_down, 1, 0)
        cdf = 0.5 * (1.0 + lax.erf(a_in * (0.5**0.5)))
        gelu = a_in * cdf
        slope = cdf + a_in * (jnp.exp(-0.5 * a_in * a_in) * 0.3989422804014327)
        act_ref[step] = (gelu * gate).astype(BF16)
        g_act = (grad_act * gate * slope).astype(BF16)
        g_gate = (grad_act * gelu).astype(BF16)
        gh_ref[step, 0] = g_act
        gh_ref[step, 1] = g_gate
        part = dot(g_act, w_act, 1, 1) + dot(g_gate, w_gate, 1, 1)
        if step == 0:
            dn[...] = part
        else:
            dn[...] += part
    for r in range(count):
        dn_refs[r][...] = dn[r * ROWS : (r + 1) * ROWS, :].astype(BF16)


MLP_SPEC = pl.BlockSpec((16, 3, 64, PAD), lambda p: (0, 0, 0, 0))
MORE_SPEC = pl.BlockSpec((16, 3, 64, PAD), lambda p: (0, 1, 0, 0))
DOWN_SPEC = pl.BlockSpec((16, 1, 64, PAD), lambda p: (0, 2, 0, 0))
DOWN_MORE_SPEC = pl.BlockSpec((16, 1, 64, PAD), lambda p: (0, 5, 0, 0))


def act_spec(count):
    return pl.BlockSpec((1, count * ROWS, PAD), lambda p: (p, 0, 0))


def hidden_spec(count):
    return pl.BlockSpec((1, 2, count * ROWS, PAD), lambda p: (p, 0, 0, 0))


def mlp(row_blocks, back_blocks, weights):
    count = len(row_blocks)
    group = count * ROWS
    return pl.pallas_call(
        functools.partial(mlp_kernel, count),
        grid=(1,),
        in_specs=[whole(ROWS, WIDTH)] * (2 * count) + [MLP_SPEC, MORE_SPEC],
        out_specs=[whole(PRE, group, PAD), whole(PRE, 2, group, PAD)]
        + [whole(ROWS, WIDTH)] * count,
        out_shape=[
            jax.ShapeDtypeStruct((PRE, group, PAD), BF16),
            jax.ShapeDtypeStruct((PRE, 2, group, PAD), BF16),
        ]
        + [jax.ShapeDtypeStruct((ROWS, WIDTH), BF16)] * count,
        scratch_shapes=[
            pltpu.VMEM((group, WIDTH), BF16),
            pltpu.VMEM((group, WIDTH), BF16),
            pltpu.VMEM((group, WIDTH), F32),
        ],
        compiler_params=pltpu.CompilerParams(vmem_limit_bytes=VMEM),
        cost_estimate=pl.CostEstimate(
            flops=5_000_000_000, bytes_accessed=8_000_000, transcendentals=500_000
        ),
        name="mlp",
    )(*row_blocks, *back_blocks, weights, weights)


def mlp_grads_kernel(*refs):
    row_refs, back_refs = refs[:M], refs[M : 2 * M]
    w0_ref, w1_ref, act0_ref, act1_ref, gh0_ref, gh1_ref, grad_ref = refs[2 * M : 2 * M + 7]
    sum_refs = refs[2 * M + 7 : 3 * M + 7]
    rows, back, sums = refs[3 * M + 7 :]
    step = pl.program_id(0)
    half = M // 2 * ROWS

    @pl.when(step == 0)
    def _():
        for r in range(M):
            rows[:, r * ROWS : (r + 1) * ROWS] = row_refs[r][...].T
            back[:, r * ROWS : (r + 1) * ROWS] = back_refs[r][...].T
        w_down = w0_ref[...].reshape(WIDTH, PAD)
        sums[:half] = dot(act0_ref[0], w_down, 1, 1)
        sums[half:] = dot(act1_ref[0], w_down, 1, 1)

    act = jnp.concatenate([act0_ref[0], act1_ref[0]], axis=0)
    for c in range(2):
        grad_hidden = jnp.concatenate([gh0_ref[0, c], gh1_ref[0, c]], axis=0)
        store_by_owner(grad_ref, c, dot(rows[...], grad_hidden, 1, 0))
    store_by_owner(grad_ref, 2, dot(back[...], act, 1, 0))

    @pl.when(step == 1)
    def _():
        w_down = w1_ref[...].reshape(WIDTH, PAD)
        sums[:half] += dot(act0_ref[0], w_down, 1, 1)
        sums[half:] += dot(act1_ref[0], w_down, 1, 1)
        for r in range(M):
            sum_refs[r][...] = sums[r * ROWS : (r + 1) * ROWS, :].astype(BF16)


def mlp_grads(row_blocks, back_blocks, weights, acts, grads_hidden):
    group = M * ROWS
    return pl.pallas_call(
        mlp_grads_kernel,
        grid=(PRE,),
        in_specs=[whole(ROWS, WIDTH)] * (2 * M)
        + [DOWN_SPEC, DOWN_MORE_SPEC]
        + [act_spec(M // 2)] * 2
        + [hidden_spec(M // 2)] * 2,
        out_specs=[pl.BlockSpec((8, 2, 3, 64, PAD), lambda p: (0, 0, p, 0, 0))]
        + [whole(ROWS, WIDTH)] * M,
        out_shape=[jax.ShapeDtypeStruct((8, 2, 3 * PRE + 3, 64, PAD), BF16)]
        + [jax.ShapeDtypeStruct((ROWS, WIDTH), BF16)] * M,
        scratch_shapes=[
            pltpu.VMEM((WIDTH, group), BF16),
            pltpu.VMEM((WIDTH, group), BF16),
            pltpu.VMEM((group, WIDTH), F32),
        ],
        compiler_params=pltpu.CompilerParams(vmem_limit_bytes=VMEM),
        cost_estimate=pl.CostEstimate(
            flops=8_000_000_000, bytes_accessed=12_000_000, transcendentals=0
        ),
        name="mlp_grads",
    )(*row_blocks, *back_blocks, weights, weights, *acts, *grads_hidden)


def out_grads_kernel(g_ref, mixed_ref, held_ref, grad_ref):
    del held_ref
    turned = g_ref[...].T
    for b in range(3):
        columns = mixed_ref[:, b * PAD : (b + 1) * PAD]
        store_by_owner(grad_ref, b, dot(turned, columns, 1, 0))


def out_grads(grad_attn, mixed_own, grads):
    return pl.pallas_call(
        out_grads_kernel,
        grid=(1,),
        in_specs=[whole(ROWS, WIDTH), whole(ROWS, 3 * PAD), pl.BlockSpec(memory_space=pl.ANY)],
        out_specs=pl.BlockSpec((8, 2, 3, 64, PAD), lambda p: (0, 0, PRE, 0, 0)),
        out_shape=jax.ShapeDtypeStruct(grads.shape, BF16),
        input_output_aliases={2: 0},
        compiler_params=pltpu.CompilerParams(vmem_limit_bytes=VMEM),
        cost_estimate=pl.CostEstimate(
            flops=400_000_000, bytes_accessed=4_000_000, transcendentals=0
        ),
        name="out_grads",
    )(grad_attn, mixed_own, grads)


def two_parts(value):
    high = value.astype(BF16)
    return high, (value - high.astype(F32)).astype(BF16)


def on_device(tokens, gain_attn, w_qkv, w_out, gain_mlp, w_in, w_down, cotangent):
    partner_tokens = exchange(tokens, PRE_AX, PRE, 1)
    w_out_later, partner_tokens = lax.optimization_barrier((w_out, partner_tokens))
    own_mlp = jnp.concatenate([w_in, w_down[:, None, :]], axis=1).transpose(1, 0, 2)
    own_mlp = jnp.pad(own_mlp, ((0, 0), (0, 0), (0, PAD - FFB)))
    own_qkv = w_qkv.reshape(64, PAD)
    out_wide = lax.all_to_all(jnp.broadcast_to(w_out_later[None], (8, 64, 2 * HD)), TP, 0, 0)
    out_wide = out_wide.transpose(1, 0, 2).reshape(64, WIDTH)
    out_wide = jnp.concatenate([out_wide, jnp.zeros((64, 2 * HD), BF16), own_qkv], axis=1)
    out_wide = out_wide.reshape(64, 4, PAD).transpose(1, 0, 2)
    weights = lax.all_gather(out_wide, FS, axis=0)
    own_mlp, out_wide = lax.optimization_barrier((own_mlp, out_wide))
    partner_mlp = exchange(own_mlp, PRE_AX, PRE, 1)
    cosine, sine = rope_tables()

    resid = tokens.astype(F32)
    hat_attn, scale_attn = normalize(resid)
    normed_attn = (hat_attn * gain_attn).astype(BF16)
    partner_rows = normalize(partner_tokens.astype(F32))[0] * gain_attn
    partner_rows = partner_rows.astype(BF16)
    first = lax.axis_index("zh") == 0
    pair = jnp.stack(
        [
            jnp.where(first, normed_attn, partner_rows),
            jnp.where(first, partner_rows, normed_attn),
        ]
    )
    rows = lax.all_to_all(jnp.broadcast_to(pair[None], (M, PRE, ROWS, WIDTH)), MLP_AX, 0, 0)
    rows = rows.reshape(8, ROWS, WIDTH)
    partner_mlp, rows = lax.optimization_barrier((partner_mlp, rows))
    weights_mlp = lax.all_gather(jnp.concatenate([own_mlp, partner_mlp], axis=0), FS, axis=0)

    cotangent_later, rows = lax.optimization_barrier((cotangent, rows))
    back_blocks = gather_by_mask(cotangent_later, MLP_AX, M)
    q, k, v, mixed, lse = attend(rows, weights, cosine, sine)
    mixed, *back_blocks = lax.optimization_barrier((mixed, *back_blocks))
    mixed_own = lax.all_to_all(mixed.reshape(8, ROWS, 2 * HD), TP, 0, 0)
    mixed_own = mixed_own.transpose(1, 0, 2).reshape(ROWS, WIDTH)
    mixed_own = jnp.pad(mixed_own, ((0, 0), (0, 3 * PAD - WIDTH)))
    full_out = [weights[:, b].reshape(WIDTH, PAD) for b in range(3)]
    attn_sum = sum(
        dot(mixed_own[:, b * PAD : (b + 1) * PAD], full_out[b], 1, 1) for b in range(3)
    )
    resid_mid = resid + attn_sum
    hat_mlp, scale_mlp = normalize(resid_mid)
    normed_mlp = (hat_mlp * gain_mlp).astype(BF16)

    row_blocks = gather_by_mask(normed_mlp, MLP_AX, M)
    act0, hidden0, *dn0 = mlp(row_blocks[:2], back_blocks[:2], weights_mlp)
    *later, dn0[1] = lax.optimization_barrier((*row_blocks[2:], dn0[1]))
    row_blocks = row_blocks[:2] + later
    act1, hidden1, *dn1 = mlp(row_blocks[2:], back_blocks[2:], weights_mlp)
    grad_normed_mlp = total(scatter_by_mask(dn0 + dn1, MLP_AX, M))
    grads, *sum_parts = mlp_grads(
        row_blocks, back_blocks, weights_mlp, (act0, act1), (hidden0, hidden1)
    )

    grad_mid_norm, gain_mlp_part = norm_back(grad_normed_mlp, hat_mlp, scale_mlp, gain_mlp)
    grad_mid = cotangent.astype(F32) + grad_mid_norm
    grad_attn = grad_mid.astype(BF16)
    grad_mixed = jnp.concatenate([dot(grad_attn, full_out[b], 1, 0) for b in range(3)], axis=1)
    grad_mixed = grad_mixed[:, :WIDTH].astype(BF16)
    gm_parts = grad_mixed.reshape(ROWS, 8, 2 * HD).transpose(1, 0, 2)
    grads = out_grads(grad_attn, mixed_own, grads)
    grads = lax.psum_scatter(grads, ("x", "c"), scatter_dimension=0)
    gm_own = lax.all_to_all(gm_parts, TP, 0, 0).reshape(LEN, 2 * HD)

    *sum_parts, gm_own = lax.optimization_barrier((*sum_parts, gm_own))
    sum_parts = scatter_by_mask(sum_parts, MLP_AX, M)
    me = lax.axis_index(TP).astype(jnp.int32)[None]
    grad_qkv, *dn_attn_parts = attend_back(
        me, q, k, v, lse, gm_own, cosine, sine, weights
    )
    held = lax.optimization_barrier((*sum_parts, *dn_attn_parts))
    sum_parts, dn_attn_parts = held[:M], held[M:]
    layer_out = (resid_mid + total(sum_parts)).astype(BF16)
    received = scatter_by_mask(dn_attn_parts, TP, 8)

    qkv_part = qkv_grads(rows, grad_qkv)
    high, low = two_parts(gain_mlp_part.reshape(16, 1, 64))
    extra = jnp.pad(jnp.concatenate([high, low], axis=1), ((0, 0), (0, 14), (0, PAD - 64)))
    got = lax.all_to_all(jnp.concatenate([qkv_part, extra], axis=1), FS, 0, 0)
    got = jnp.sum(got.astype(F32), axis=0)
    grad_qkv_w = got[:64]
    gain_mlp_own = got[64, :64] + got[65, :64]
    gain_own = lax.dynamic_slice_in_dim(gain_attn, lax.axis_index(FS) * 64, 64)
    gain_attn_own = jnp.sum(grad_qkv_w * own_qkv.astype(F32), axis=1) / gain_own
    gains = jnp.concatenate([gain_attn_own, gain_mlp_own])
    bit = lax.axis_index("zl")
    keep = lax.dynamic_index_in_dim(grads, bit, 0, keepdims=False)
    send = lax.dynamic_index_in_dim(grads, 1 - bit, 0, keepdims=False)
    halves = keep.astype(F32) + exchange(send, ("zl",), 2, 1).astype(F32)
    from_partner = exchange(halves[3:6].astype(BF16), PRE_AX, PRE, 1)
    grad_mlp = halves[:3] + from_partner.astype(F32)
    grad_in = grad_mlp[:2, :, :FFB].transpose(1, 0, 2)
    grad_down = grad_mlp[2, :, :FFB]
    out_parts = halves[6:].astype(BF16).transpose(1, 0, 2).reshape(64, 3 * PAD)[:, :WIDTH]
    out_parts = out_parts.reshape(64, 8, 2 * HD).transpose(1, 0, 2)
    gains = jnp.broadcast_to(gains[None, None], (128, 1, 128))
    gains = lax.all_to_all(gains, AXES, 0, 0).reshape(16, 8, 128).sum(axis=1)
    grad_out = jnp.sum(lax.all_to_all(out_parts, TP, 0, 0).astype(F32), axis=0)

    grad_normed_attn = total(received)
    grad_first, _ = norm_back(grad_normed_attn, hat_attn, scale_attn, gain_attn)
    grad_tokens = (grad_mid + grad_first).astype(BF16)
    return (
        layer_out,
        grad_tokens,
        gains[:, :64].reshape(WIDTH),
        grad_qkv_w.reshape(64, 3, 2 * HD),
        grad_out,
        gains[:, 64:].reshape(WIDTH),
        grad_in,
        grad_down,
    )


def solution(mesh):
    fine = Mesh(mesh.devices.reshape(4, 2, 2, 2, 2, 2), AXES)
    in_specs = (
        P(AXES, None),
        P(),
        P(FS, None, TP),
        P(FS, TP),
        P(),
        P(FS, None, TP),
        P(FS, TP),
        P(AXES, None),
    )
    out_specs = (
        P(AXES, None),
        P(AXES, None),
        P(),
        P(FS, None, TP),
        P(FS, TP),
        P(),
        P(FS, None, TP),
        P(FS, TP),
    )
    return jax.shard_map(
        on_device, mesh=fine, in_specs=in_specs, out_specs=out_specs, check_vma=False
    )
```

```python
import functools

import jax
import jax.numpy as jnp
import numpy as np
from jax import lax
from jax.experimental import pallas as pl
from jax.experimental.pallas import tpu as pltpu
from jax.sharding import Mesh
from jax.sharding import PartitionSpec as P

HD = 64
LEN = 1280
EPSILON = 1e-05
THETA = 160000.0
ROWS = 160
WIDTH = 1024
FFB = 328
PAD = 384
QB = 256
BACK_QB = 320
VMEM = 60 * 1024 * 1024

AXES = ("x", "zl", "c", "yh", "yl", "zh")
FS = ("x", "zl", "c")
TP = ("yh", "yl", "zh")
MLP_AX = ("yh", "yl")
PRE_AX = ("zh",)
M = 4
PRE = 2
F32 = jnp.float32
BF16 = jnp.bfloat16


def exchange(value, axes, count, mask):
    return lax.ppermute(value, axes, [(i, i ^ mask) for i in range(count)])


def gather_by_mask(value, axes, count):
    return [value] + [exchange(value, axes, count, m) for m in range(1, count)]


def scatter_by_mask(parts, axes, count):
    return [parts[0]] + [exchange(parts[m], axes, count, m) for m in range(1, count)]


def total(parts):
    result = parts[0].astype(F32)
    for part in parts[1:]:
        result = result + part.astype(F32)
    return result


def normalize(values):
    centre = values - jnp.mean(values, axis=-1, keepdims=True)
    scaling = lax.rsqrt(jnp.mean(centre * centre, axis=-1, keepdims=True) + EPSILON)
    return (centre * scaling, scaling)


def norm_back(grad_normed, normed_hat, scaling, gain):
    grad_hat = grad_normed * gain
    mean_grad = jnp.mean(grad_hat, axis=-1, keepdims=True)
    mean_proj = jnp.mean(grad_hat * normed_hat, axis=-1, keepdims=True)
    return (
        scaling * (grad_hat - mean_grad - normed_hat * mean_proj),
        jnp.sum(grad_normed * normed_hat, axis=0),
    )


def rope_tables():
    half = HD // 2
    freqs = THETA ** (-np.arange(half) * 2.0 / HD)
    angles = np.arange(LEN)[:, None] * freqs[None, :]
    cosine, sine = np.cos(angles), np.sin(angles)
    return (
        jnp.asarray(np.concatenate([cosine] * 4, axis=1), F32),
        jnp.asarray(np.concatenate([-sine, sine, -sine, sine], axis=1), F32),
    )


def by_head(values):
    lane = lax.broadcasted_iota(jnp.int32, values.shape, 1)
    zeros = jnp.zeros_like(values)
    return jnp.concatenate(
        [jnp.where(lane < HD, values, zeros), jnp.where(lane < HD, zeros, values)], axis=0
    )


def dot(a, b, ca, cb):
    return lax.dot_general(a, b, (((ca,), (cb,)), ((), ())), preferred_element_type=F32)


def swap_halves(values):
    lane = lax.broadcasted_iota(jnp.int32, values.shape, 1)
    first = (lane // 32) % 2 == 0
    return jnp.where(first, pltpu.roll(values, 96, 1), pltpu.roll(values, 32, 1))


def head_mask(values, head):
    lane = lax.broadcasted_iota(jnp.int32, values.shape, 1)
    return jnp.where((lane // HD) == head, values, jnp.zeros_like(values))


def attend_kernel(
    rows_ref, w_ref, cos_ref, sin_ref, q_ref, k_ref, v_ref, mixed_ref, lse_ref, proj
):
    proj[...] = dot(rows_ref[...].reshape(LEN, WIDTH), w_ref[...].reshape(WIDTH, PAD), 1, 0)
    cosine, sine = cos_ref[...], sin_ref[...]
    value = proj[:, : 2 * HD]
    value = value * cosine + swap_halves(value) * sine
    q_ref[...] = value.astype(BF16) * jnp.asarray(0.125, BF16)
    value = proj[:, 2 * HD : 4 * HD]
    k_ref[...] = (value * cosine + swap_halves(value) * sine).astype(BF16)
    v_ref[...] = proj[:, 4 * HD :].astype(BF16)

    def block(i, carry):
        at = pl.ds(pl.multiple_of(i * QB, QB), QB)
        query = q_ref[at, :]
        outs = []
        sums = []
        for head in range(2):
            scores = dot(head_mask(query, head), k_ref[...], 1, 1)
            peak = jnp.max(scores, axis=1, keepdims=True)
            exponent = jnp.exp(scores - peak)
            row_sum = jnp.sum(exponent, axis=1, keepdims=True)
            out = dot(exponent.astype(BF16), v_ref[...], 1, 0)
            outs.append(out / row_sum)
            sums.append(jnp.broadcast_to(peak + jnp.log(row_sum), (QB, 2 * HD)))
        lane = lax.broadcasted_iota(jnp.int32, (QB, 2 * HD), 1)
        mixed_ref[at, :] = jnp.where(lane < HD, outs[0], outs[1]).astype(BF16)
        lse_ref[at, :] = jnp.where(lane < HD, sums[0], sums[1])
        return carry

    lax.fori_loop(0, LEN // QB, block, 0)


def whole(*shape):
    return pl.BlockSpec(shape, lambda i: (0,) * len(shape))


ROWS_SPEC = pl.BlockSpec((8, ROWS, WIDTH), lambda i: (0, 0, 0))
QKV_SPEC = pl.BlockSpec((16, 1, 64, PAD), lambda i: (0, 3, 0, 0))


def attend(rows, weights, cosine, sine):
    wide = jax.ShapeDtypeStruct((LEN, 2 * HD), BF16)
    return pl.pallas_call(
        attend_kernel,
        grid=(1,),
        in_specs=[ROWS_SPEC, QKV_SPEC, whole(LEN, 2 * HD), whole(LEN, 2 * HD)],
        out_specs=[whole(LEN, 2 * HD)] * 5,
        out_shape=[wide, wide, wide, wide, jax.ShapeDtypeStruct((LEN, 2 * HD), F32)],
        scratch_shapes=[pltpu.VMEM((LEN, PAD), F32)],
        compiler_params=pltpu.CompilerParams(vmem_limit_bytes=VMEM),
        cost_estimate=pl.CostEstimate(
            flops=6_000_000_000, bytes_accessed=8_000_000, transcendentals=3_300_000
        ),
        name="attend",
    )(rows, weights, cosine, sine)


def attend_back_kernel(me_ref, *refs):
    q_ref, k_ref, v_ref, lse_ref, g_ref, cos_ref, sin_ref, w_ref, out_ref = refs[:9]
    dn_refs = refs[9:17]
    key_sum, val_sum, dn = refs[17:]
    key_sum[...] = jnp.zeros_like(key_sum)
    val_sum[...] = jnp.zeros_like(val_sum)

    def block(i, carry):
        at = pl.ds(pl.multiple_of(i * BACK_QB, BACK_QB), BACK_QB)
        query = by_head(q_ref[at, :])
        grad = by_head(g_ref[at, :])
        logs = jnp.concatenate([lse_ref[at, :1], lse_ref[at, HD : HD + 1]], axis=0)
        probs = jnp.exp(dot(query, k_ref[...], 1, 1) - logs)
        grad_probs = dot(grad, v_ref[...], 1, 1)
        inner = jnp.sum(grad_probs * probs, axis=1, keepdims=True)
        grad_scores = (probs * (grad_probs - inner)).astype(BF16)
        both = dot(grad_scores, k_ref[...], 1, 0)
        lane = lax.broadcasted_iota(jnp.int32, (BACK_QB, 2 * HD), 1)
        grad_query = jnp.where(lane < HD, both[:BACK_QB], both[BACK_QB:])
        key_sum[...] += dot(query, grad_scores, 0, 0)
        val_sum[...] += dot(grad, probs.astype(BF16), 0, 0)
        grad_query = grad_query * 0.125
        cosine, sine = cos_ref[at, :], sin_ref[at, :]
        grad_query = grad_query * cosine - swap_halves(grad_query) * sine
        out_ref[at, : 2 * HD] = grad_query.astype(BF16)
        return carry

    lax.fori_loop(0, LEN // BACK_QB, block, 0)
    grad_key = key_sum[...].T
    grad_key = grad_key * cos_ref[...] - swap_halves(grad_key) * sin_ref[...]
    out_ref[:, 2 * HD : 4 * HD] = grad_key.astype(BF16)
    out_ref[:, 4 * HD :] = val_sum[...].T.astype(BF16)
    dn[...] = dot(out_ref[...], w_ref[...].reshape(WIDTH, PAD), 1, 1).astype(BF16)
    me = me_ref[0]
    for m in range(8):
        at = pl.multiple_of(jnp.bitwise_xor(me, m) * ROWS, ROWS)
        dn_refs[m][...] = dn[pl.ds(at, ROWS), :]


def attend_back(me, q, k, v, lse, grad_mixed, cosine, sine, weights):
    return pl.pallas_call(
        attend_back_kernel,
        grid=(1,),
        in_specs=[pl.BlockSpec(memory_space=pltpu.SMEM)]
        + [whole(LEN, 2 * HD)] * 7
        + [QKV_SPEC],
        out_specs=[whole(LEN, PAD)] + [whole(ROWS, WIDTH)] * 8,
        out_shape=[jax.ShapeDtypeStruct((LEN, PAD), BF16)]
        + [jax.ShapeDtypeStruct((ROWS, WIDTH), BF16)] * 8,
        scratch_shapes=[
            pltpu.VMEM((2 * HD, LEN), F32),
            pltpu.VMEM((2 * HD, LEN), F32),
            pltpu.VMEM((LEN, WIDTH), BF16),
        ],
        compiler_params=pltpu.CompilerParams(vmem_limit_bytes=VMEM),
        cost_estimate=pl.CostEstimate(
            flops=12_000_000_000, bytes_accessed=8_000_000, transcendentals=3_300_000
        ),
        name="attend_back",
    )(me, q, k, v, lse, grad_mixed, cosine, sine, weights)


def qkv_grads_kernel(rows_ref, g_ref, out_ref, turned):
    for r in range(8):
        turned[:, r * ROWS : (r + 1) * ROWS] = rows_ref[r].T
    out_ref[...] = dot(turned[...], g_ref[...], 1, 0).astype(BF16).reshape(16, 64, PAD)


def qkv_grads(rows, grad_qkv):
    return pl.pallas_call(
        qkv_grads_kernel,
        grid=(1,),
        in_specs=[ROWS_SPEC, whole(LEN, PAD)],
        out_specs=whole(16, 64, PAD),
        out_shape=jax.ShapeDtypeStruct((16, 64, PAD), BF16),
        scratch_shapes=[pltpu.VMEM((WIDTH, LEN), BF16)],
        compiler_params=pltpu.CompilerParams(vmem_limit_bytes=VMEM),
        cost_estimate=pl.CostEstimate(
            flops=2_000_000_000, bytes_accessed=5_000_000, transcendentals=0
        ),
        name="qkv_grads",
    )(rows, grad_qkv)


def store_by_owner(ref, at, value):
    value = value.astype(BF16)
    for x in range(4):
        for zl in range(2):
            for c in range(2):
                row = (x * 4 + zl * 2 + c) * 64
                ref[x * 2 + c, zl, at] = value[row : row + 64, :]


def mlp_kernel(count, *refs):
    row_refs, back_refs = refs[:count], refs[count : 2 * count]
    w0_ref, w1_ref, act_ref, gh_ref = refs[2 * count : 2 * count + 4]
    dn_refs = refs[2 * count + 4 : 3 * count + 4]
    rows, back, dn = refs[3 * count + 4 :]
    for r in range(count):
        rows[r * ROWS : (r + 1) * ROWS, :] = row_refs[r][...]
        back[r * ROWS : (r + 1) * ROWS, :] = back_refs[r][...]
    for step, w_ref in enumerate((w0_ref, w1_ref)):
        w_act = w_ref[:, 0].reshape(WIDTH, PAD)
        w_gate = w_ref[:, 1].reshape(WIDTH, PAD)
        w_down = w_ref[:, 2].reshape(WIDTH, PAD)
        a_in = dot(rows[...], w_act, 1, 0)
        gate = dot(rows[...], w_gate, 1, 0)
        grad_act = dot(back[...], w_down, 1, 0)
        cdf = 0.5 * (1.0 + lax.erf(a_in * (0.5**0.5)))
        gelu = a_in * cdf
        slope = cdf + a_in * (jnp.exp(-0.5 * a_in * a_in) * 0.3989422804014327)
        act_ref[step] = (gelu * gate).astype(BF16)
        g_act = (grad_act * gate * slope).astype(BF16)
        g_gate = (grad_act * gelu).astype(BF16)
        gh_ref[step, 0] = g_act
        gh_ref[step, 1] = g_gate
        part = dot(g_act, w_act, 1, 1) + dot(g_gate, w_gate, 1, 1)
        if step == 0:
            dn[...] = part
        else:
            dn[...] += part
    for r in range(count):
        dn_refs[r][...] = dn[r * ROWS : (r + 1) * ROWS, :].astype(BF16)


MLP_SPEC = pl.BlockSpec((16, 3, 64, PAD), lambda p: (0, 0, 0, 0))
MORE_SPEC = pl.BlockSpec((16, 3, 64, PAD), lambda p: (0, 1, 0, 0))
DOWN_SPEC = pl.BlockSpec((16, 1, 64, PAD), lambda p: (0, 2, 0, 0))
DOWN_MORE_SPEC = pl.BlockSpec((16, 1, 64, PAD), lambda p: (0, 5, 0, 0))


def act_spec(count):
    return pl.BlockSpec((1, count * ROWS, PAD), lambda p: (p, 0, 0))


def hidden_spec(count):
    return pl.BlockSpec((1, 2, count * ROWS, PAD), lambda p: (p, 0, 0, 0))


def mlp(row_blocks, back_blocks, weights):
    count = len(row_blocks)
    group = count * ROWS
    return pl.pallas_call(
        functools.partial(mlp_kernel, count),
        grid=(1,),
        in_specs=[whole(ROWS, WIDTH)] * (2 * count) + [MLP_SPEC, MORE_SPEC],
        out_specs=[whole(PRE, group, PAD), whole(PRE, 2, group, PAD)]
        + [whole(ROWS, WIDTH)] * count,
        out_shape=[
            jax.ShapeDtypeStruct((PRE, group, PAD), BF16),
            jax.ShapeDtypeStruct((PRE, 2, group, PAD), BF16),
        ]
        + [jax.ShapeDtypeStruct((ROWS, WIDTH), BF16)] * count,
        scratch_shapes=[
            pltpu.VMEM((group, WIDTH), BF16),
            pltpu.VMEM((group, WIDTH), BF16),
            pltpu.VMEM((group, WIDTH), F32),
        ],
        compiler_params=pltpu.CompilerParams(vmem_limit_bytes=VMEM),
        cost_estimate=pl.CostEstimate(
            flops=5_000_000_000, bytes_accessed=8_000_000, transcendentals=500_000
        ),
        name="mlp",
    )(*row_blocks, *back_blocks, weights, weights)


def mlp_grads_kernel(*refs):
    row_refs, back_refs = refs[:M], refs[M : 2 * M]
    w0_ref, w1_ref, act0_ref, act1_ref, gh0_ref, gh1_ref, grad_ref = refs[2 * M : 2 * M + 7]
    sum_refs = refs[2 * M + 7 : 3 * M + 7]
    rows, back, sums = refs[3 * M + 7 :]
    step = pl.program_id(0)
    half = M // 2 * ROWS

    @pl.when(step == 0)
    def _():
        for r in range(M):
            rows[:, r * ROWS : (r + 1) * ROWS] = row_refs[r][...].T
            back[:, r * ROWS : (r + 1) * ROWS] = back_refs[r][...].T
        w_down = w0_ref[...].reshape(WIDTH, PAD)
        sums[:half] = dot(act0_ref[0], w_down, 1, 1)
        sums[half:] = dot(act1_ref[0], w_down, 1, 1)

    act = jnp.concatenate([act0_ref[0], act1_ref[0]], axis=0)
    for c in range(2):
        grad_hidden = jnp.concatenate([gh0_ref[0, c], gh1_ref[0, c]], axis=0)
        store_by_owner(grad_ref, c, dot(rows[...], grad_hidden, 1, 0))
    store_by_owner(grad_ref, 2, dot(back[...], act, 1, 0))

    @pl.when(step == 1)
    def _():
        w_down = w1_ref[...].reshape(WIDTH, PAD)
        sums[:half] += dot(act0_ref[0], w_down, 1, 1)
        sums[half:] += dot(act1_ref[0], w_down, 1, 1)
        for r in range(M):
            sum_refs[r][...] = sums[r * ROWS : (r + 1) * ROWS, :].astype(BF16)


def mlp_grads(row_blocks, back_blocks, weights, acts, grads_hidden):
    group = M * ROWS
    return pl.pallas_call(
        mlp_grads_kernel,
        grid=(PRE,),
        in_specs=[whole(ROWS, WIDTH)] * (2 * M)
        + [DOWN_SPEC, DOWN_MORE_SPEC]
        + [act_spec(M // 2)] * 2
        + [hidden_spec(M // 2)] * 2,
        out_specs=[pl.BlockSpec((8, 2, 3, 64, PAD), lambda p: (0, 0, p, 0, 0))]
        + [whole(ROWS, WIDTH)] * M,
        out_shape=[jax.ShapeDtypeStruct((8, 2, 3 * PRE + 3, 64, PAD), BF16)]
        + [jax.ShapeDtypeStruct((ROWS, WIDTH), BF16)] * M,
        scratch_shapes=[
            pltpu.VMEM((WIDTH, group), BF16),
            pltpu.VMEM((WIDTH, group), BF16),
            pltpu.VMEM((group, WIDTH), F32),
        ],
        compiler_params=pltpu.CompilerParams(vmem_limit_bytes=VMEM),
        cost_estimate=pl.CostEstimate(
            flops=8_000_000_000, bytes_accessed=12_000_000, transcendentals=0
        ),
        name="mlp_grads",
    )(*row_blocks, *back_blocks, weights, weights, *acts, *grads_hidden)


def out_grads_kernel(g_ref, mixed_ref, held_ref, grad_ref):
    del held_ref
    turned = g_ref[...].T
    for b in range(3):
        columns = mixed_ref[:, b * PAD : (b + 1) * PAD]
        store_by_owner(grad_ref, b, dot(turned, columns, 1, 0))


def out_grads(grad_attn, mixed_own, grads):
    return pl.pallas_call(
        out_grads_kernel,
        grid=(1,),
        in_specs=[whole(ROWS, WIDTH), whole(ROWS, 3 * PAD), pl.BlockSpec(memory_space=pl.ANY)],
        out_specs=pl.BlockSpec((8, 2, 3, 64, PAD), lambda p: (0, 0, PRE, 0, 0)),
        out_shape=jax.ShapeDtypeStruct(grads.shape, BF16),
        input_output_aliases={2: 0},
        compiler_params=pltpu.CompilerParams(vmem_limit_bytes=VMEM),
        cost_estimate=pl.CostEstimate(
            flops=400_000_000, bytes_accessed=4_000_000, transcendentals=0
        ),
        name="out_grads",
    )(grad_attn, mixed_own, grads)


def two_parts(value):
    high = value.astype(BF16)
    return high, (value - high.astype(F32)).astype(BF16)


def on_device(tokens, gain_attn, w_qkv, w_out, gain_mlp, w_in, w_down, cotangent):
    partner_tokens = exchange(tokens, PRE_AX, PRE, 1)
    w_out_later, partner_tokens = lax.optimization_barrier((w_out, partner_tokens))
    own_mlp = jnp.concatenate([w_in, w_down[:, None, :]], axis=1).transpose(1, 0, 2)
    own_mlp = jnp.pad(own_mlp, ((0, 0), (0, 0), (0, PAD - FFB)))
    own_qkv = w_qkv.reshape(64, PAD)
    out_wide = lax.all_to_all(jnp.broadcast_to(w_out_later[None], (8, 64, 2 * HD)), TP, 0, 0)
    out_wide = out_wide.transpose(1, 0, 2).reshape(64, WIDTH)
    out_wide = jnp.concatenate([out_wide, jnp.zeros((64, 2 * HD), BF16), own_qkv], axis=1)
    out_wide = out_wide.reshape(64, 4, PAD).transpose(1, 0, 2)
    weights = lax.all_gather(out_wide, FS, axis=0)
    own_mlp, out_wide = lax.optimization_barrier((own_mlp, out_wide))
    partner_mlp = exchange(own_mlp, PRE_AX, PRE, 1)
    cosine, sine = rope_tables()

    resid = tokens.astype(F32)
    hat_attn, scale_attn = normalize(resid)
    normed_attn = (hat_attn * gain_attn).astype(BF16)
    partner_rows = normalize(partner_tokens.astype(F32))[0] * gain_attn
    partner_rows = partner_rows.astype(BF16)
    first = lax.axis_index("zh") == 0
    pair = jnp.stack(
        [
            jnp.where(first, normed_attn, partner_rows),
            jnp.where(first, partner_rows, normed_attn),
        ]
    )
    rows = lax.all_to_all(jnp.broadcast_to(pair[None], (M, PRE, ROWS, WIDTH)), MLP_AX, 0, 0)
    rows = rows.reshape(8, ROWS, WIDTH)
    partner_mlp, rows = lax.optimization_barrier((partner_mlp, rows))
    weights_mlp = lax.all_gather(jnp.concatenate([own_mlp, partner_mlp], axis=0), FS, axis=0)

    cotangent_later, rows = lax.optimization_barrier((cotangent, rows))
    back_blocks = gather_by_mask(cotangent_later, MLP_AX, M)
    q, k, v, mixed, lse = attend(rows, weights, cosine, sine)
    mixed, *back_blocks = lax.optimization_barrier((mixed, *back_blocks))
    mixed_own = lax.all_to_all(mixed.reshape(8, ROWS, 2 * HD), TP, 0, 0)
    mixed_own = mixed_own.transpose(1, 0, 2).reshape(ROWS, WIDTH)
    mixed_own = jnp.pad(mixed_own, ((0, 0), (0, 3 * PAD - WIDTH)))
    full_out = [weights[:, b].reshape(WIDTH, PAD) for b in range(3)]
    attn_sum = sum(
        dot(mixed_own[:, b * PAD : (b + 1) * PAD], full_out[b], 1, 1) for b in range(3)
    )
    resid_mid = resid + attn_sum
    hat_mlp, scale_mlp = normalize(resid_mid)
    normed_mlp = (hat_mlp * gain_mlp).astype(BF16)

    row_blocks = gather_by_mask(normed_mlp, MLP_AX, M)
    act0, hidden0, *dn0 = mlp(row_blocks[:2], back_blocks[:2], weights_mlp)
    *later, dn0[1] = lax.optimization_barrier((*row_blocks[2:], dn0[1]))
    row_blocks = row_blocks[:2] + later
    act1, hidden1, *dn1 = mlp(row_blocks[2:], back_blocks[2:], weights_mlp)
    grad_normed_mlp = total(scatter_by_mask(dn0 + dn1, MLP_AX, M))
    grads, *sum_parts = mlp_grads(
        row_blocks, back_blocks, weights_mlp, (act0, act1), (hidden0, hidden1)
    )

    grad_mid_norm, gain_mlp_part = norm_back(grad_normed_mlp, hat_mlp, scale_mlp, gain_mlp)
    grad_mid = cotangent.astype(F32) + grad_mid_norm
    grad_attn = grad_mid.astype(BF16)
    grad_mixed = jnp.concatenate([dot(grad_attn, full_out[b], 1, 0) for b in range(3)], axis=1)
    grad_mixed = grad_mixed[:, :WIDTH].astype(BF16)
    gm_parts = grad_mixed.reshape(ROWS, 8, 2 * HD).transpose(1, 0, 2)
    grad_attn_later, gm_parts = lax.optimization_barrier((grad_attn, gm_parts))
    grads = out_grads(grad_attn_later, mixed_own, grads)
    grads = lax.psum_scatter(grads, ("x", "c"), scatter_dimension=0)
    gm_own = lax.all_to_all(gm_parts, TP, 0, 0).reshape(LEN, 2 * HD)

    *sum_parts, gm_own = lax.optimization_barrier((*sum_parts, gm_own))
    sum_parts = scatter_by_mask(sum_parts, MLP_AX, M)
    me = lax.axis_index(TP).astype(jnp.int32)[None]
    grad_qkv, *dn_attn_parts = attend_back(
        me, q, k, v, lse, gm_own, cosine, sine, weights
    )
    held = lax.optimization_barrier((*sum_parts, *dn_attn_parts))
    sum_parts, dn_attn_parts = held[:M], held[M:]
    layer_out = (resid_mid + total(sum_parts)).astype(BF16)
    received = scatter_by_mask(dn_attn_parts, TP, 8)

    qkv_part = qkv_grads(rows, grad_qkv)
    high, low = two_parts(gain_mlp_part.reshape(16, 1, 64))
    extra = jnp.pad(jnp.concatenate([high, low], axis=1), ((0, 0), (0, 14), (0, PAD - 64)))
    got = lax.all_to_all(jnp.concatenate([qkv_part, extra], axis=1), FS, 0, 0)
    got = jnp.sum(got.astype(F32), axis=0)
    grad_qkv_w = got[:64]
    gain_mlp_own = got[64, :64] + got[65, :64]
    gain_own = lax.dynamic_slice_in_dim(gain_attn, lax.axis_index(FS) * 64, 64)
    gain_attn_own = jnp.sum(grad_qkv_w * own_qkv.astype(F32), axis=1) / gain_own
    gains = jnp.concatenate([gain_attn_own, gain_mlp_own])
    bit = lax.axis_index("zl")
    keep = lax.dynamic_index_in_dim(grads, bit, 0, keepdims=False)
    send = lax.dynamic_index_in_dim(grads, 1 - bit, 0, keepdims=False)
    halves = keep.astype(F32) + exchange(send, ("zl",), 2, 1).astype(F32)
    from_partner = exchange(halves[3:6].astype(BF16), PRE_AX, PRE, 1)
    grad_mlp = halves[:3] + from_partner.astype(F32)
    grad_in = grad_mlp[:2, :, :FFB].transpose(1, 0, 2)
    grad_down = grad_mlp[2, :, :FFB]
    out_parts = halves[6:].astype(BF16).transpose(1, 0, 2).reshape(64, 3 * PAD)[:, :WIDTH]
    out_parts = out_parts.reshape(64, 8, 2 * HD).transpose(1, 0, 2)
    gains = jnp.broadcast_to(gains[None, None], (128, 1, 128))
    gains = lax.all_to_all(gains, AXES, 0, 0).reshape(16, 8, 128).sum(axis=1)
    grad_out = jnp.sum(lax.all_to_all(out_parts, TP, 0, 0).astype(F32), axis=0)

    grad_normed_attn = total(received)
    grad_first, _ = norm_back(grad_normed_attn, hat_attn, scale_attn, gain_attn)
    grad_tokens = (grad_mid + grad_first).astype(BF16)
    return (
        layer_out,
        grad_tokens,
        gains[:, :64].reshape(WIDTH),
        grad_qkv_w.reshape(64, 3, 2 * HD),
        grad_out,
        gains[:, 64:].reshape(WIDTH),
        grad_in,
        grad_down,
    )


def solution(mesh):
    fine = Mesh(mesh.devices.reshape(4, 2, 2, 2, 2, 2), AXES)
    in_specs = (
        P(AXES, None),
        P(),
        P(FS, None, TP),
        P(FS, TP),
        P(),
        P(FS, None, TP),
        P(FS, TP),
        P(AXES, None),
    )
    out_specs = (
        P(AXES, None),
        P(AXES, None),
        P(),
        P(FS, None, TP),
        P(FS, TP),
        P(),
        P(FS, None, TP),
        P(FS, TP),
    )
    return jax.shard_map(
        on_device, mesh=fine, in_specs=in_specs, out_specs=out_specs, check_vma=False
    )
```

```python
import functools

import jax
import jax.numpy as jnp
import numpy as np
from jax import lax
from jax.experimental import pallas as pl
from jax.experimental.pallas import tpu as pltpu
from jax.sharding import Mesh
from jax.sharding import PartitionSpec as P

HD = 64
LEN = 1280
EPSILON = 1e-05
THETA = 160000.0
ROWS = 160
WIDTH = 1024
FFB = 328
PAD = 384
QB = 320
BACK_QB = 320
VMEM = 60 * 1024 * 1024

AXES = ("x", "zl", "c", "yh", "yl", "zh")
FS = ("x", "zl", "c")
TP = ("yh", "yl", "zh")
MLP_AX = ("yh", "yl")
PRE_AX = ("zh",)
M = 4
PRE = 2
F32 = jnp.float32
BF16 = jnp.bfloat16


def exchange(value, axes, count, mask):
    return lax.ppermute(value, axes, [(i, i ^ mask) for i in range(count)])


def gather_by_mask(value, axes, count):
    return [value] + [exchange(value, axes, count, m) for m in range(1, count)]


def scatter_by_mask(parts, axes, count):
    return [parts[0]] + [exchange(parts[m], axes, count, m) for m in range(1, count)]


def total(parts):
    result = parts[0].astype(F32)
    for part in parts[1:]:
        result = result + part.astype(F32)
    return result


def normalize(values):
    centre = values - jnp.mean(values, axis=-1, keepdims=True)
    scaling = lax.rsqrt(jnp.mean(centre * centre, axis=-1, keepdims=True) + EPSILON)
    return (centre * scaling, scaling)


def norm_back(grad_normed, normed_hat, scaling, gain):
    grad_hat = grad_normed * gain
    mean_grad = jnp.mean(grad_hat, axis=-1, keepdims=True)
    mean_proj = jnp.mean(grad_hat * normed_hat, axis=-1, keepdims=True)
    return (
        scaling * (grad_hat - mean_grad - normed_hat * mean_proj),
        jnp.sum(grad_normed * normed_hat, axis=0),
    )


def rope_tables():
    half = HD // 2
    freqs = THETA ** (-np.arange(half) * 2.0 / HD)
    angles = np.arange(LEN)[:, None] * freqs[None, :]
    cosine, sine = np.cos(angles), np.sin(angles)
    return (
        jnp.asarray(np.concatenate([cosine] * 4, axis=1), F32),
        jnp.asarray(np.concatenate([-sine, sine, -sine, sine], axis=1), F32),
    )


def by_head(values):
    lane = lax.broadcasted_iota(jnp.int32, values.shape, 1)
    zeros = jnp.zeros_like(values)
    return jnp.concatenate(
        [jnp.where(lane < HD, values, zeros), jnp.where(lane < HD, zeros, values)], axis=0
    )


def dot(a, b, ca, cb):
    return lax.dot_general(a, b, (((ca,), (cb,)), ((), ())), preferred_element_type=F32)


def swap_halves(values):
    lane = lax.broadcasted_iota(jnp.int32, values.shape, 1)
    first = (lane // 32) % 2 == 0
    return jnp.where(first, pltpu.roll(values, 96, 1), pltpu.roll(values, 32, 1))


def head_mask(values, head):
    lane = lax.broadcasted_iota(jnp.int32, values.shape, 1)
    return jnp.where((lane // HD) == head, values, jnp.zeros_like(values))


def attend_kernel(
    rows_ref, w_ref, cos_ref, sin_ref, q_ref, k_ref, v_ref, mixed_ref, lse_ref, proj
):
    proj[...] = dot(rows_ref[...].reshape(LEN, WIDTH), w_ref[...].reshape(WIDTH, PAD), 1, 0)
    cosine, sine = cos_ref[...], sin_ref[...]
    value = proj[:, : 2 * HD]
    value = value * cosine + swap_halves(value) * sine
    q_ref[...] = value.astype(BF16) * jnp.asarray(0.125, BF16)
    value = proj[:, 2 * HD : 4 * HD]
    k_ref[...] = (value * cosine + swap_halves(value) * sine).astype(BF16)
    v_ref[...] = proj[:, 4 * HD :].astype(BF16)

    def block(i, carry):
        at = pl.ds(pl.multiple_of(i * QB, QB), QB)
        query = q_ref[at, :]
        outs = []
        sums = []
        for head in range(2):
            scores = dot(head_mask(query, head), k_ref[...], 1, 1)
            peak = jnp.max(scores, axis=1, keepdims=True)
            exponent = jnp.exp(scores - peak)
            row_sum = jnp.sum(exponent, axis=1, keepdims=True)
            out = dot(exponent.astype(BF16), v_ref[...], 1, 0)
            outs.append(out / row_sum)
            sums.append(jnp.broadcast_to(peak + jnp.log(row_sum), (QB, 2 * HD)))
        lane = lax.broadcasted_iota(jnp.int32, (QB, 2 * HD), 1)
        mixed_ref[at, :] = jnp.where(lane < HD, outs[0], outs[1]).astype(BF16)
        lse_ref[at, :] = jnp.where(lane < HD, sums[0], sums[1])
        return carry

    lax.fori_loop(0, LEN // QB, block, 0)


def whole(*shape):
    return pl.BlockSpec(shape, lambda i: (0,) * len(shape))


ROWS_SPEC = pl.BlockSpec((8, ROWS, WIDTH), lambda i: (0, 0, 0))
QKV_SPEC = pl.BlockSpec((16, 1, 64, PAD), lambda i: (0, 3, 0, 0))


def attend(rows, weights, cosine, sine):
    wide = jax.ShapeDtypeStruct((LEN, 2 * HD), BF16)
    return pl.pallas_call(
        attend_kernel,
        grid=(1,),
        in_specs=[ROWS_SPEC, QKV_SPEC, whole(LEN, 2 * HD), whole(LEN, 2 * HD)],
        out_specs=[whole(LEN, 2 * HD)] * 5,
        out_shape=[wide, wide, wide, wide, jax.ShapeDtypeStruct((LEN, 2 * HD), F32)],
        scratch_shapes=[pltpu.VMEM((LEN, PAD), F32)],
        compiler_params=pltpu.CompilerParams(vmem_limit_bytes=VMEM),
        cost_estimate=pl.CostEstimate(
            flops=6_000_000_000, bytes_accessed=8_000_000, transcendentals=3_300_000
        ),
        name="attend",
    )(rows, weights, cosine, sine)


def attend_back_kernel(me_ref, *refs):
    q_ref, k_ref, v_ref, lse_ref, g_ref, cos_ref, sin_ref, w_ref, out_ref = refs[:9]
    dn_refs = refs[9:17]
    key_sum, val_sum, dn = refs[17:]
    key_sum[...] = jnp.zeros_like(key_sum)
    val_sum[...] = jnp.zeros_like(val_sum)

    def block(i, carry):
        at = pl.ds(pl.multiple_of(i * BACK_QB, BACK_QB), BACK_QB)
        query = by_head(q_ref[at, :])
        grad = by_head(g_ref[at, :])
        logs = jnp.concatenate([lse_ref[at, :1], lse_ref[at, HD : HD + 1]], axis=0)
        probs = jnp.exp(dot(query, k_ref[...], 1, 1) - logs)
        grad_probs = dot(grad, v_ref[...], 1, 1)
        inner = jnp.sum(grad_probs * probs, axis=1, keepdims=True)
        grad_scores = (probs * (grad_probs - inner)).astype(BF16)
        both = dot(grad_scores, k_ref[...], 1, 0)
        lane = lax.broadcasted_iota(jnp.int32, (BACK_QB, 2 * HD), 1)
        grad_query = jnp.where(lane < HD, both[:BACK_QB], both[BACK_QB:])
        key_sum[...] += dot(query, grad_scores, 0, 0)
        val_sum[...] += dot(grad, probs.astype(BF16), 0, 0)
        grad_query = grad_query * 0.125
        cosine, sine = cos_ref[at, :], sin_ref[at, :]
        grad_query = grad_query * cosine - swap_halves(grad_query) * sine
        out_ref[at, : 2 * HD] = grad_query.astype(BF16)
        return carry

    lax.fori_loop(0, LEN // BACK_QB, block, 0)
    grad_key = key_sum[...].T
    grad_key = grad_key * cos_ref[...] - swap_halves(grad_key) * sin_ref[...]
    out_ref[:, 2 * HD : 4 * HD] = grad_key.astype(BF16)
    out_ref[:, 4 * HD :] = val_sum[...].T.astype(BF16)
    dn[...] = dot(out_ref[...], w_ref[...].reshape(WIDTH, PAD), 1, 1).astype(BF16)
    me = me_ref[0]
    for m in range(8):
        at = pl.multiple_of(jnp.bitwise_xor(me, m) * ROWS, ROWS)
        dn_refs[m][...] = dn[pl.ds(at, ROWS), :]


def attend_back(me, q, k, v, lse, grad_mixed, cosine, sine, weights):
    return pl.pallas_call(
        attend_back_kernel,
        grid=(1,),
        in_specs=[pl.BlockSpec(memory_space=pltpu.SMEM)]
        + [whole(LEN, 2 * HD)] * 7
        + [QKV_SPEC],
        out_specs=[whole(LEN, PAD)] + [whole(ROWS, WIDTH)] * 8,
        out_shape=[jax.ShapeDtypeStruct((LEN, PAD), BF16)]
        + [jax.ShapeDtypeStruct((ROWS, WIDTH), BF16)] * 8,
        scratch_shapes=[
            pltpu.VMEM((2 * HD, LEN), F32),
            pltpu.VMEM((2 * HD, LEN), F32),
            pltpu.VMEM((LEN, WIDTH), BF16),
        ],
        compiler_params=pltpu.CompilerParams(vmem_limit_bytes=VMEM),
        cost_estimate=pl.CostEstimate(
            flops=12_000_000_000, bytes_accessed=8_000_000, transcendentals=3_300_000
        ),
        name="attend_back",
    )(me, q, k, v, lse, grad_mixed, cosine, sine, weights)


def qkv_grads_kernel(rows_ref, g_ref, out_ref, turned):
    for r in range(8):
        turned[:, r * ROWS : (r + 1) * ROWS] = rows_ref[r].T
    out_ref[...] = dot(turned[...], g_ref[...], 1, 0).astype(BF16).reshape(16, 64, PAD)


def qkv_grads(rows, grad_qkv):
    return pl.pallas_call(
        qkv_grads_kernel,
        grid=(1,),
        in_specs=[ROWS_SPEC, whole(LEN, PAD)],
        out_specs=whole(16, 64, PAD),
        out_shape=jax.ShapeDtypeStruct((16, 64, PAD), BF16),
        scratch_shapes=[pltpu.VMEM((WIDTH, LEN), BF16)],
        compiler_params=pltpu.CompilerParams(vmem_limit_bytes=VMEM),
        cost_estimate=pl.CostEstimate(
            flops=2_000_000_000, bytes_accessed=5_000_000, transcendentals=0
        ),
        name="qkv_grads",
    )(rows, grad_qkv)


def store_by_owner(ref, at, value):
    value = value.astype(BF16)
    for x in range(4):
        for zl in range(2):
            for c in range(2):
                row = (x * 4 + zl * 2 + c) * 64
                ref[x * 2 + c, zl, at] = value[row : row + 64, :]


def mlp_kernel(count, *refs):
    row_refs, back_refs = refs[:count], refs[count : 2 * count]
    w0_ref, w1_ref, act_ref, gh_ref = refs[2 * count : 2 * count + 4]
    dn_refs = refs[2 * count + 4 : 3 * count + 4]
    rows, back, dn = refs[3 * count + 4 :]
    for r in range(count):
        rows[r * ROWS : (r + 1) * ROWS, :] = row_refs[r][...]
        back[r * ROWS : (r + 1) * ROWS, :] = back_refs[r][...]
    for step, w_ref in enumerate((w0_ref, w1_ref)):
        w_act = w_ref[:, 0].reshape(WIDTH, PAD)
        w_gate = w_ref[:, 1].reshape(WIDTH, PAD)
        w_down = w_ref[:, 2].reshape(WIDTH, PAD)
        a_in = dot(rows[...], w_act, 1, 0)
        gate = dot(rows[...], w_gate, 1, 0)
        grad_act = dot(back[...], w_down, 1, 0)
        cdf = 0.5 * (1.0 + lax.erf(a_in * (0.5**0.5)))
        gelu = a_in * cdf
        slope = cdf + a_in * (jnp.exp(-0.5 * a_in * a_in) * 0.3989422804014327)
        act_ref[step] = (gelu * gate).astype(BF16)
        g_act = (grad_act * gate * slope).astype(BF16)
        g_gate = (grad_act * gelu).astype(BF16)
        gh_ref[step, 0] = g_act
        gh_ref[step, 1] = g_gate
        part = dot(g_act, w_act, 1, 1) + dot(g_gate, w_gate, 1, 1)
        if step == 0:
            dn[...] = part
        else:
            dn[...] += part
    for r in range(count):
        dn_refs[r][...] = dn[r * ROWS : (r + 1) * ROWS, :].astype(BF16)


MLP_SPEC = pl.BlockSpec((16, 3, 64, PAD), lambda p: (0, 0, 0, 0))
MORE_SPEC = pl.BlockSpec((16, 3, 64, PAD), lambda p: (0, 1, 0, 0))
DOWN_SPEC = pl.BlockSpec((16, 1, 64, PAD), lambda p: (0, 2, 0, 0))
DOWN_MORE_SPEC = pl.BlockSpec((16, 1, 64, PAD), lambda p: (0, 5, 0, 0))


def act_spec(count):
    return pl.BlockSpec((1, count * ROWS, PAD), lambda p: (p, 0, 0))


def hidden_spec(count):
    return pl.BlockSpec((1, 2, count * ROWS, PAD), lambda p: (p, 0, 0, 0))


def mlp(row_blocks, back_blocks, weights):
    count = len(row_blocks)
    group = count * ROWS
    return pl.pallas_call(
        functools.partial(mlp_kernel, count),
        grid=(1,),
        in_specs=[whole(ROWS, WIDTH)] * (2 * count) + [MLP_SPEC, MORE_SPEC],
        out_specs=[whole(PRE, group, PAD), whole(PRE, 2, group, PAD)]
        + [whole(ROWS, WIDTH)] * count,
        out_shape=[
            jax.ShapeDtypeStruct((PRE, group, PAD), BF16),
            jax.ShapeDtypeStruct((PRE, 2, group, PAD), BF16),
        ]
        + [jax.ShapeDtypeStruct((ROWS, WIDTH), BF16)] * count,
        scratch_shapes=[
            pltpu.VMEM((group, WIDTH), BF16),
            pltpu.VMEM((group, WIDTH), BF16),
            pltpu.VMEM((group, WIDTH), F32),
        ],
        compiler_params=pltpu.CompilerParams(vmem_limit_bytes=VMEM),
        cost_estimate=pl.CostEstimate(
            flops=5_000_000_000, bytes_accessed=8_000_000, transcendentals=500_000
        ),
        name="mlp",
    )(*row_blocks, *back_blocks, weights, weights)


def mlp_grads_kernel(*refs):
    row_refs, back_refs = refs[:M], refs[M : 2 * M]
    w0_ref, w1_ref, act0_ref, act1_ref, gh0_ref, gh1_ref, grad_ref = refs[2 * M : 2 * M + 7]
    sum_refs = refs[2 * M + 7 : 3 * M + 7]
    rows, back, sums = refs[3 * M + 7 :]
    step = pl.program_id(0)
    half = M // 2 * ROWS

    @pl.when(step == 0)
    def _():
        for r in range(M):
            rows[:, r * ROWS : (r + 1) * ROWS] = row_refs[r][...].T
            back[:, r * ROWS : (r + 1) * ROWS] = back_refs[r][...].T
        w_down = w0_ref[...].reshape(WIDTH, PAD)
        sums[:half] = dot(act0_ref[0], w_down, 1, 1)
        sums[half:] = dot(act1_ref[0], w_down, 1, 1)

    act = jnp.concatenate([act0_ref[0], act1_ref[0]], axis=0)
    for c in range(2):
        grad_hidden = jnp.concatenate([gh0_ref[0, c], gh1_ref[0, c]], axis=0)
        store_by_owner(grad_ref, c, dot(rows[...], grad_hidden, 1, 0))
    store_by_owner(grad_ref, 2, dot(back[...], act, 1, 0))

    @pl.when(step == 1)
    def _():
        w_down = w1_ref[...].reshape(WIDTH, PAD)
        sums[:half] += dot(act0_ref[0], w_down, 1, 1)
        sums[half:] += dot(act1_ref[0], w_down, 1, 1)
        for r in range(M):
            sum_refs[r][...] = sums[r * ROWS : (r + 1) * ROWS, :].astype(BF16)


def mlp_grads(row_blocks, back_blocks, weights, acts, grads_hidden):
    group = M * ROWS
    return pl.pallas_call(
        mlp_grads_kernel,
        grid=(PRE,),
        in_specs=[whole(ROWS, WIDTH)] * (2 * M)
        + [DOWN_SPEC, DOWN_MORE_SPEC]
        + [act_spec(M // 2)] * 2
        + [hidden_spec(M // 2)] * 2,
        out_specs=[pl.BlockSpec((8, 2, 3, 64, PAD), lambda p: (0, 0, p, 0, 0))]
        + [whole(ROWS, WIDTH)] * M,
        out_shape=[jax.ShapeDtypeStruct((8, 2, 3 * PRE + 3, 64, PAD), BF16)]
        + [jax.ShapeDtypeStruct((ROWS, WIDTH), BF16)] * M,
        scratch_shapes=[
            pltpu.VMEM((WIDTH, group), BF16),
            pltpu.VMEM((WIDTH, group), BF16),
            pltpu.VMEM((group, WIDTH), F32),
        ],
        compiler_params=pltpu.CompilerParams(vmem_limit_bytes=VMEM),
        cost_estimate=pl.CostEstimate(
            flops=8_000_000_000, bytes_accessed=12_000_000, transcendentals=0
        ),
        name="mlp_grads",
    )(*row_blocks, *back_blocks, weights, weights, *acts, *grads_hidden)


def out_grads_kernel(g_ref, mixed_ref, held_ref, grad_ref):
    del held_ref
    turned = g_ref[...].T
    for b in range(3):
        columns = mixed_ref[:, b * PAD : (b + 1) * PAD]
        store_by_owner(grad_ref, b, dot(turned, columns, 1, 0))


def out_grads(grad_attn, mixed_own, grads):
    return pl.pallas_call(
        out_grads_kernel,
        grid=(1,),
        in_specs=[whole(ROWS, WIDTH), whole(ROWS, 3 * PAD), pl.BlockSpec(memory_space=pl.ANY)],
        out_specs=pl.BlockSpec((8, 2, 3, 64, PAD), lambda p: (0, 0, PRE, 0, 0)),
        out_shape=jax.ShapeDtypeStruct(grads.shape, BF16),
        input_output_aliases={2: 0},
        compiler_params=pltpu.CompilerParams(vmem_limit_bytes=VMEM),
        cost_estimate=pl.CostEstimate(
            flops=400_000_000, bytes_accessed=4_000_000, transcendentals=0
        ),
        name="out_grads",
    )(grad_attn, mixed_own, grads)


def two_parts(value):
    high = value.astype(BF16)
    return high, (value - high.astype(F32)).astype(BF16)


def on_device(tokens, gain_attn, w_qkv, w_out, gain_mlp, w_in, w_down, cotangent):
    partner_tokens = exchange(tokens, PRE_AX, PRE, 1)
    w_out_later, partner_tokens = lax.optimization_barrier((w_out, partner_tokens))
    own_mlp = jnp.concatenate([w_in, w_down[:, None, :]], axis=1).transpose(1, 0, 2)
    own_mlp = jnp.pad(own_mlp, ((0, 0), (0, 0), (0, PAD - FFB)))
    own_qkv = w_qkv.reshape(64, PAD)
    out_wide = lax.all_to_all(jnp.broadcast_to(w_out_later[None], (8, 64, 2 * HD)), TP, 0, 0)
    out_wide = out_wide.transpose(1, 0, 2).reshape(64, WIDTH)
    out_wide = jnp.concatenate([out_wide, jnp.zeros((64, 2 * HD), BF16), own_qkv], axis=1)
    out_wide = out_wide.reshape(64, 4, PAD).transpose(1, 0, 2)
    weights = lax.all_gather(out_wide, FS, axis=0)
    own_mlp, out_wide = lax.optimization_barrier((own_mlp, out_wide))
    partner_mlp = exchange(own_mlp, PRE_AX, PRE, 1)
    cosine, sine = rope_tables()

    resid = tokens.astype(F32)
    hat_attn, scale_attn = normalize(resid)
    normed_attn = (hat_attn * gain_attn).astype(BF16)
    partner_rows = normalize(partner_tokens.astype(F32))[0] * gain_attn
    partner_rows = partner_rows.astype(BF16)
    first = lax.axis_index("zh") == 0
    pair = jnp.stack(
        [
            jnp.where(first, normed_attn, partner_rows),
            jnp.where(first, partner_rows, normed_attn),
        ]
    )
    rows = lax.all_to_all(jnp.broadcast_to(pair[None], (M, PRE, ROWS, WIDTH)), MLP_AX, 0, 0)
    rows = rows.reshape(8, ROWS, WIDTH)
    partner_mlp, rows = lax.optimization_barrier((partner_mlp, rows))
    weights_mlp = lax.all_gather(jnp.concatenate([own_mlp, partner_mlp], axis=0), FS, axis=0)

    cotangent_later, rows = lax.optimization_barrier((cotangent, rows))
    back_blocks = gather_by_mask(cotangent_later, MLP_AX, M)
    q, k, v, mixed, lse = attend(rows, weights, cosine, sine)
    mixed, *back_blocks = lax.optimization_barrier((mixed, *back_blocks))
    mixed_own = lax.all_to_all(mixed.reshape(8, ROWS, 2 * HD), TP, 0, 0)
    mixed_own = mixed_own.transpose(1, 0, 2).reshape(ROWS, WIDTH)
    mixed_own = jnp.pad(mixed_own, ((0, 0), (0, 3 * PAD - WIDTH)))
    full_out = [weights[:, b].reshape(WIDTH, PAD) for b in range(3)]
    attn_sum = sum(
        dot(mixed_own[:, b * PAD : (b + 1) * PAD], full_out[b], 1, 1) for b in range(3)
    )
    resid_mid = resid + attn_sum
    hat_mlp, scale_mlp = normalize(resid_mid)
    normed_mlp = (hat_mlp * gain_mlp).astype(BF16)

    row_blocks = gather_by_mask(normed_mlp, MLP_AX, M)
    act0, hidden0, *dn0 = mlp(row_blocks[:2], back_blocks[:2], weights_mlp)
    *later, dn0[1] = lax.optimization_barrier((*row_blocks[2:], dn0[1]))
    row_blocks = row_blocks[:2] + later
    act1, hidden1, *dn1 = mlp(row_blocks[2:], back_blocks[2:], weights_mlp)
    grad_normed_mlp = total(scatter_by_mask(dn0 + dn1, MLP_AX, M))
    grads, *sum_parts = mlp_grads(
        row_blocks, back_blocks, weights_mlp, (act0, act1), (hidden0, hidden1)
    )

    grad_mid_norm, gain_mlp_part = norm_back(grad_normed_mlp, hat_mlp, scale_mlp, gain_mlp)
    grad_mid = cotangent.astype(F32) + grad_mid_norm
    grad_attn = grad_mid.astype(BF16)
    grad_mixed = jnp.concatenate([dot(grad_attn, full_out[b], 1, 0) for b in range(3)], axis=1)
    grad_mixed = grad_mixed[:, :WIDTH].astype(BF16)
    gm_parts = grad_mixed.reshape(ROWS, 8, 2 * HD).transpose(1, 0, 2)
    grad_attn_later, gm_parts = lax.optimization_barrier((grad_attn, gm_parts))
    grads = out_grads(grad_attn_later, mixed_own, grads)
    grads = lax.psum_scatter(grads, ("x", "c"), scatter_dimension=0)
    gm_own = lax.all_to_all(gm_parts, TP, 0, 0).reshape(LEN, 2 * HD)

    *sum_parts, gm_own = lax.optimization_barrier((*sum_parts, gm_own))
    sum_parts = scatter_by_mask(sum_parts, MLP_AX, M)
    me = lax.axis_index(TP).astype(jnp.int32)[None]
    grad_qkv, *dn_attn_parts = attend_back(
        me, q, k, v, lse, gm_own, cosine, sine, weights
    )
    held = lax.optimization_barrier((*sum_parts, *dn_attn_parts))
    sum_parts, dn_attn_parts = held[:M], held[M:]
    layer_out = (resid_mid + total(sum_parts)).astype(BF16)
    received = scatter_by_mask(dn_attn_parts, TP, 8)

    qkv_part = qkv_grads(rows, grad_qkv)
    high, low = two_parts(gain_mlp_part.reshape(16, 1, 64))
    extra = jnp.pad(jnp.concatenate([high, low], axis=1), ((0, 0), (0, 14), (0, PAD - 64)))
    got = lax.all_to_all(jnp.concatenate([qkv_part, extra], axis=1), FS, 0, 0)
    got = jnp.sum(got.astype(F32), axis=0)
    grad_qkv_w = got[:64]
    gain_mlp_own = got[64, :64] + got[65, :64]
    gain_own = lax.dynamic_slice_in_dim(gain_attn, lax.axis_index(FS) * 64, 64)
    gain_attn_own = jnp.sum(grad_qkv_w * own_qkv.astype(F32), axis=1) / gain_own
    gains = jnp.concatenate([gain_attn_own, gain_mlp_own])
    bit = lax.axis_index("zl")
    keep = lax.dynamic_index_in_dim(grads, bit, 0, keepdims=False)
    send = lax.dynamic_index_in_dim(grads, 1 - bit, 0, keepdims=False)
    halves = keep.astype(F32) + exchange(send, ("zl",), 2, 1).astype(F32)
    from_partner = exchange(halves[3:6].astype(BF16), PRE_AX, PRE, 1)
    grad_mlp = halves[:3] + from_partner.astype(F32)
    grad_in = grad_mlp[:2, :, :FFB].transpose(1, 0, 2)
    grad_down = grad_mlp[2, :, :FFB]
    out_parts = halves[6:].astype(BF16).transpose(1, 0, 2).reshape(64, 3 * PAD)[:, :WIDTH]
    out_parts = out_parts.reshape(64, 8, 2 * HD).transpose(1, 0, 2)
    gains = jnp.broadcast_to(gains[None, None], (128, 1, 128))
    gains = lax.all_to_all(gains, AXES, 0, 0).reshape(16, 8, 128).sum(axis=1)
    grad_out = jnp.sum(lax.all_to_all(out_parts, TP, 0, 0).astype(F32), axis=0)

    grad_normed_attn = total(received)
    grad_first, _ = norm_back(grad_normed_attn, hat_attn, scale_attn, gain_attn)
    grad_tokens = (grad_mid + grad_first).astype(BF16)
    return (
        layer_out,
        grad_tokens,
        gains[:, :64].reshape(WIDTH),
        grad_qkv_w.reshape(64, 3, 2 * HD),
        grad_out,
        gains[:, 64:].reshape(WIDTH),
        grad_in,
        grad_down,
    )


def solution(mesh):
    fine = Mesh(mesh.devices.reshape(4, 2, 2, 2, 2, 2), AXES)
    in_specs = (
        P(AXES, None),
        P(),
        P(FS, None, TP),
        P(FS, TP),
        P(),
        P(FS, None, TP),
        P(FS, TP),
        P(AXES, None),
    )
    out_specs = (
        P(AXES, None),
        P(AXES, None),
        P(),
        P(FS, None, TP),
        P(FS, TP),
        P(),
        P(FS, None, TP),
        P(FS, TP),
    )
    return jax.shard_map(
        on_device, mesh=fine, in_specs=in_specs, out_specs=out_specs, check_vma=False
    )
```
